128 devices in a mesh: seq: 16 (over x, z), head: 8 (over y, core).
Axes of the slice: x: 4, y: 4, z: 4, core: 2. Of those that a mesh axis runs over, the one named last changes fastest.
Arguments:
- hidden_states: bfloat16 [65536, 2048], P('seq'), may hold values from -40 to 40
- w_query: bfloat16 [2048, 2048], P('seq', 'head'), may hold values from -1 to 1
- w_key: bfloat16 [2048, 2048], P('seq', 'head'), may hold values from -1 to 1
- w_value: bfloat16 [2048, 2048], P('seq', 'head'), may hold values from -1 to 1
- norm_gain: float32 [2048], P('head'), may hold values from 0.1 to 1.9
Outputs:
- normed_out: bfloat16 [65536, 2048], P('seq', 'head')
The draws below stay inside these ranges and needn't reach their ends.
All inputs are finite; a program needn't handle non-finite values.
Results may differ from the reference program's by a relative error of at most 0.007.
Values may be sent and summed in bfloat16 or wider, within the bound.
No kernel may reach another device: no remote copies, remote signals or barrier semaphores. Data moves between devices by JAX's collectives and lax.ppermute only.
A program may use at most 128 MiB of HBM per device.

```python
import jax
import jax.numpy as jnp
from jax import lax

D = 2048
H = 16
DH = 128
B = 128
LEVELS = 7
TOKENS = 65536


def common_weight(key):
    return jax.random.normal(key, (D, H * DH), jnp.float32) * D ** (-0.5)


def draw_hidden_states(key, part):
    key = jax.random.fold_in(key, 11)
    summed_field = jnp.zeros((TOKENS, D), jnp.float32)
    for coarse in range(8):
        amplitude = 0.5 if coarse == 0 else 0.35
        rough = jax.random.normal(jax.random.fold_in(key, coarse), (TOKENS // 2 ** coarse, D), jnp.float32)
        summed_field = summed_field + amplitude * jnp.repeat(rough, 2 ** coarse, axis=0)
    return jnp.clip(summed_field, -40.0, 40.0).astype(jnp.bfloat16)


def draw_w_query(key, part):
    shared = common_weight(key)
    return jnp.clip(shared, -1.0, 1.0).astype(jnp.bfloat16)


def draw_w_key(key, part):
    key = jax.random.fold_in(key, 22)
    own_part = jax.random.normal(key, (D, H * DH), jnp.float32) * D ** (-0.5)
    mixed = own_part
    return jnp.clip(mixed, -1.0, 1.0).astype(jnp.bfloat16)


def draw_w_value(key, part):
    key = jax.random.fold_in(key, 23)
    own_part = jax.random.normal(key, (D, H * DH), jnp.float32) * D ** (-0.5)
    head_number = (jnp.arange(H * DH) // DH).astype(jnp.float32)
    rising = 1.0 + 2.0 * head_number / (H - 1)
    factor = jnp.sqrt(rising)
    return jnp.clip(own_part * factor[None, :], -1.0, 1.0).astype(jnp.bfloat16)


def setup_inputs(seed: int = 0) -> dict:
    seeds = jax.random.split(jax.random.key(seed), 6)
    return {
        "hidden_states": draw_hidden_states(jax.random.fold_in(seeds[5], 71), 0),
        "w_query": draw_w_query(jax.random.fold_in(seeds[5], 71), 0),
        "w_key": draw_w_key(jax.random.fold_in(seeds[5], 71), 0),
        "w_value": draw_w_value(jax.random.fold_in(seeds[5], 71), 0),
        "norm_gain": jnp.clip(1.0 + 0.18 * jax.random.normal(seeds[4], (H * DH,), jnp.float32), 0.1, 1.9),
    }


def attend(queries, key_rows, values, visible, scaling):
    scores = jnp.einsum('nqd,nkd->nqk', queries.astype(jnp.float32), key_rows.astype(jnp.float32)) * scaling
    if visible is not None:
        scores = jnp.where(visible[:, None, :], scores, -jnp.inf)
    highest = lax.optimization_barrier(jnp.max(scores, axis=-1))
    weights = jnp.exp(scores - highest[..., None])
    row_total = lax.optimization_barrier(jnp.sum(weights, axis=-1))
    rounded = lax.optimization_barrier(weights.astype(jnp.bfloat16)).astype(jnp.float32)
    weighted = jnp.einsum('nqk,nkd->nqd', rounded, values.astype(jnp.float32))
    return (highest, weighted, row_total)

def head_levels(queries, key_rows, value_rows):
    length = queries.shape[0]
    block_count = length // B
    scaling = DH ** (-0.5)
    zero_rows = jnp.zeros((B, DH), jnp.bfloat16)

    def windows(member):
        padded = jnp.concatenate([zero_rows, member, zero_rows], axis=0)
        return jnp.concatenate([padded[:-2 * B].reshape(block_count, B, DH), padded[B:-B].reshape(block_count, B, DH), padded[2 * B:].reshape(block_count, B, DH)], axis=1)
    block_index = jnp.arange(block_count)[:, None]
    column = jnp.arange(3 * B)[None, :]
    visible = jnp.logical_not((column < B) & (block_index == 0) | (column >= 2 * B) & (block_index == block_count - 1))
    highest, weighted, row_total = attend(queries.reshape(block_count, B, DH), windows(key_rows), windows(value_rows), visible, scaling)
    results = [(1, highest.reshape(length), weighted.reshape(length, DH), row_total.reshape(length))]
    for coarse in range(1, LEVELS + 1):
        stride = 2 ** coarse
        row_count = length // stride
        pair_count = row_count // B
        pooled = [lax.optimization_barrier(jnp.mean(member.reshape(row_count, stride, DH).astype(jnp.float32), axis=1)).astype(jnp.bfloat16) for member in (queries, key_rows, value_rows)]
        query_blocks = pooled[0].reshape(pair_count, B, DH)
        key_blocks = pooled[1].reshape(pair_count // 2, 2, B, DH)[:, ::-1].reshape(pair_count, B, DH)
        value_blocks = pooled[2].reshape(pair_count // 2, 2, B, DH)[:, ::-1].reshape(pair_count, B, DH)
        highest, weighted, row_total = attend(query_blocks, key_blocks, value_blocks, None, scaling)
        results.append((stride, highest.reshape(row_count), weighted.reshape(row_count, DH), row_total.reshape(row_count)))
    overall = jnp.full((length,), -jnp.inf, jnp.float32)
    for stride, highest, weighted, row_total in results:
        overall = jnp.maximum(overall, jnp.repeat(highest, stride))
    numerator = jnp.zeros((length, DH), jnp.float32)
    denominator = jnp.zeros((length,), jnp.float32)
    for stride, highest, weighted, row_total in results:
        factor = jnp.exp(jnp.repeat(highest, stride) - overall)
        numerator = numerator + factor[:, None] * jnp.repeat(weighted, stride, axis=0)
        denominator = denominator + factor * jnp.repeat(row_total, stride)
    return numerator / denominator[:, None]

def per_head(triple):
    return head_levels(triple[0], triple[1], triple[2])

def reference(hidden_states, w_query, w_key, w_value, norm_gain):
    projected = [jnp.dot(hidden_states, weight_matrix, preferred_element_type=jnp.float32).astype(jnp.bfloat16) for weight_matrix in (w_query, w_key, w_value)]
    stacked = [member.reshape(TOKENS, H, DH).transpose(1, 0, 2) for member in projected]
    attention = lax.map(per_head, (stacked[0], stacked[1], stacked[2]))
    attention = attention.transpose(1, 0, 2).reshape(TOKENS, H * DH)
    squares = lax.optimization_barrier(jnp.sum(attention * attention, axis=1))
    scaling = lax.rsqrt(squares / (H * DH) + 1e-06)
    return (attention * scaling[:, None] * norm_gain[None, :]).astype(jnp.bfloat16)
```

```python
import jax
import jax.numpy as jnp
import numpy as np
from jax import lax
from jax.experimental import pallas as pl
from jax.experimental.pallas import tpu as pltpu
from jax.sharding import PartitionSpec as P

H = 16
DH = 128
B = 128
D = 2048
HEADS = 2
SIDE = 4
TOKENS = 4096
SCALE = float(DH**-0.5 * np.log2(np.e))
GONE = -1e30
SHIFTS = (1, 3, 2)
BF = jnp.bfloat16
F32 = jnp.float32
TM = 1024
SUB = 256


def line_perm(first, shift):
    pairs = []
    for x in range(SIDE):
        for z in range(SIDE):
            for head in range(8):
                if (head % 2 == 0) == first:
                    target = x * SIDE + (z + shift) % SIDE
                else:
                    target = (x + shift) % SIDE * SIDE + z
                pairs.append(((x * SIDE + z) * 8 + head, target * 8 + head))
    return pairs


def along_line(value, first, shift):
    return lax.ppermute(value, ("seq", "head"), line_perm(first, shift))


def flipped(value, bits):
    return lax.ppermute(value, "seq", [(i, i ^ bits) for i in range(16)])


def other_side(value):
    pairs = [(i, i + 1) for i in range(1, 15, 2)] + [(i + 1, i) for i in range(1, 15, 2)]
    return lax.ppermute(value, "seq", pairs)


def over_heads(value, step):
    return lax.ppermute(value, "head", [(i, step(i)) for i in range(8)])


def dot(a, b):
    return lax.dot_general(a, b, (((1,), (0,)), ((), ())), preferred_element_type=F32)


def dot_t(a, b):
    return lax.dot_general(a, b, (((1,), (1,)), ((), ())), preferred_element_type=F32)


def iota(shape, dim):
    return lax.broadcasted_iota(jnp.int32, shape, dim)


def level_matches(rows, first, levels, row_dim):
    shape = (128, rows) if row_dim == 1 else (rows, rows)
    token, slot = iota(shape, 0), iota(shape, 1)
    found = jnp.zeros(shape, jnp.bool_)
    start = 0
    for level in levels:
        count = 128 >> (level - first + 1)
        found = found | ((slot - start) == (token >> (level - first + 1)))  & (slot >= start) & (
            slot < start + count
        )
        start += count
    return found


def pool_matrix(rows, tokens, levels):
    row, token = iota((rows, tokens), 0), iota((rows, tokens), 1)
    total = jnp.zeros((rows, tokens), F32)
    start = 0
    for level in levels:
        count = tokens >> level
        inside = (row >= start) & (row < start + count) & ((row - start) == (token >> level))
        total = jnp.where(inside, 2.0**-level, total)
        start += count
    return total.astype(BF)


def project_kernel(
    place, h_ref, w0, w1, w2, w3, qkv, l1, l2, l3, l4, q5, q6, q7, send_a, send_b, w_all, p_fine, p_coarse
):
    step = pl.program_id(0)

    @pl.when(step == 0)
    def _():
        for outer, piece in enumerate((w0, w1, w2, w3)):
            for inner in range(SIDE):
                at = pl.multiple_of(place[outer * SIDE + inner] * 128, 128)
                w_all[pl.ds(at, 128), :] = piece[inner]
        p_fine[...] = pool_matrix(112, 128, (1, 2, 3))
        p_coarse[...] = pool_matrix(128, TM, (4, 5, 6, 7))

    @pl.loop(0, TM // SUB)
    def _(part):
        at = pl.multiple_of(part * SUB, SUB)
        rows = dot(h_ref[pl.ds(at, SUB), :], w_all[...]).astype(BF)
        qkv[pl.ds(at, SUB), :] = rows
        for half in range(SUB // 128):
            pooled = dot(p_fine[...], rows[half * 128 : half * 128 + 128]).astype(BF)
            block = part * (SUB // 128) + half
            l1[pl.ds(pl.multiple_of(block * 64, 64), 64), :] = pooled[:64]
            l2[pl.ds(pl.multiple_of(block * 32, 32), 32), :] = pooled[64:96]
            l3[pl.ds(pl.multiple_of(block * 16, 16), 16), :] = pooled[96:112]

    pooled = dot(p_coarse[...], qkv[...])
    mine = pooled.astype(BF)
    l4[...] = mine[:64]
    q5[pl.ds(pl.multiple_of(step * 32, 32), 32), :] = mine[64:96, :256]
    q6[pl.ds(pl.multiple_of(step * 16, 16), 16), :] = mine[96:112, :256]
    q7[pl.ds(pl.multiple_of(step * 8, 8), 8), :] = pooled[112:120, :256]
    send_a[pl.ds(pl.multiple_of(128 + step * 32, 32), 32), :] = mine[64:96, 256:]
    send_a[pl.ds(pl.multiple_of(256 + step * 16, 16), 16), :] = mine[96:112, 256:]
    keep = pooled[112:120, 256:]
    for run in range(TOKENS // TM):

        @pl.when(step == run)
        def _(run=run):
            if run % 2 == 0:
                send_a[320 + run * 8 : 336 + run * 8, :] = jnp.concatenate([keep, keep], 0).astype(BF)
            else:
                before = send_a[312 + run * 8 : 328 + run * 8, :].astype(F32)
                send_a[312 + run * 8 : 328 + run * 8, :] = jnp.concatenate(
                    [before[:8], keep], 0
                ).astype(BF)

    odd = place[16] == 1
    low = (step == 0) & odd
    high = (step == TOKENS // TM - 1) & jnp.logical_not(odd)

    @pl.when(step == 0)
    def _():
        edge = qkv[:128, 256:]

        @pl.when(odd)
        def _():
            send_a[:128, :] = edge

        @pl.when(jnp.logical_not(odd))
        def _():
            send_b[...] = edge

    @pl.when(step == TOKENS // TM - 1)
    def _():
        edge = qkv[TM - 128 :, 256:]

        @pl.when(odd)
        def _():
            send_b[...] = edge

        @pl.when(jnp.logical_not(odd))
        def _():
            send_a[:128, :] = edge


def project(place, hidden, pieces):
    whole = lambda shape: pl.BlockSpec(shape, lambda i, p: (0,) * len(shape))
    tiles = lambda rows, cols: pl.BlockSpec((rows, cols), lambda i, p: (i, 0))
    shape = jax.ShapeDtypeStruct
    return pl.pallas_call(
        project_kernel,
        grid_spec=pltpu.PrefetchScalarGridSpec(
            num_scalar_prefetch=1,
            grid=(TOKENS // TM,),
            in_specs=[tiles(TM, D)] + [whole((SIDE, 128, 768))] * 4,
            out_specs=[
                tiles(TM, 768),
                tiles(TM // 2, 768),
                tiles(TM // 4, 768),
                tiles(TM // 8, 768),
                tiles(TM // 16, 768),
                whole((128, 256)),
                whole((64, 256)),
                whole((32, 256)),
                whole((352, 512)),
                whole((128, 512)),
            ],
            scratch_shapes=[
                pltpu.VMEM((D, 768), BF),
                pltpu.VMEM((112, 128), BF),
                pltpu.VMEM((128, TM), BF),
            ],
        ),
        out_shape=[
            shape((TOKENS, 768), BF),
            shape((TOKENS // 2, 768), BF),
            shape((TOKENS // 4, 768), BF),
            shape((TOKENS // 8, 768), BF),
            shape((TOKENS // 16, 768), BF),
            shape((128, 256), BF),
            shape((64, 256), BF),
            shape((32, 256), F32),
            shape((352, 512), BF),
            shape((128, 512), BF),
        ],
        compiler_params=pltpu.CompilerParams(
            dimension_semantics=("arbitrary",), vmem_limit_bytes=56 * 2**20
        ),
        name="project_and_pool",
        cost_estimate=pl.CostEstimate(
            flops=2 * TOKENS * D * 768, bytes_accessed=26 * 2**20, transcendentals=0
        ),
    )(place, hidden, *pieces)


def with_ones(values):
    return jnp.concatenate([values, jnp.ones_like(values)], axis=1)


def attend(queries, key_rows, values):
    scores = dot_t(queries, key_rows) * SCALE
    highest = jnp.max(scores, axis=1, keepdims=True)
    weights = jnp.exp2(scores - highest).astype(BF)
    both = dot(weights, with_ones(values))
    total = both[:, DH:]
    return (both[:, :DH] / total).astype(BF), highest + jnp.log2(total)


def pairs_kernel(l1, l2, o1, e1, o2, e2):
    for head in range(HEADS):
        q, k, v = (slice(i * 256 + head * 128, i * 256 + head * 128 + 128) for i in range(3))
        c = slice(head * 128, head * 128 + 128)

        for block in range(4):
            mine = slice(block * 128, block * 128 + 128)
            its = slice((block ^ 1) * 128, (block ^ 1) * 128 + 128)
            o1[mine, c], e1[mine, c] = attend(l1[mine, q], l1[its, k], l1[its, v])
        for block in range(2):
            mine = slice(block * 128, block * 128 + 128)
            its = slice((block ^ 1) * 128, (block ^ 1) * 128 + 128)
            o2[mine, c], e2[mine, c] = attend(l2[mine, q], l2[its, k], l2[its, v])


def pairs(l1, l2):
    tiles = lambda rows, cols: pl.BlockSpec((rows, cols), lambda i: (i, 0))
    shape = jax.ShapeDtypeStruct
    return pl.pallas_call(
        pairs_kernel,
        grid=(4,),
        in_specs=[tiles(512, 768), tiles(256, 768)],
        out_specs=[tiles(512, 256), tiles(512, 256), tiles(256, 256), tiles(256, 256)],
        out_shape=[
            shape((2048, 256), BF),
            shape((2048, 256), F32),
            shape((1024, 256), BF),
            shape((1024, 256), F32),
        ],
        compiler_params=pltpu.CompilerParams(vmem_limit_bytes=56 * 2**20),
        name="levels_1_2",
        cost_estimate=pl.CostEstimate(
            flops=2 * 3072 * 128 * 512, bytes_accessed=9 * 2**20, transcendentals=3072 * 256
        ),
    )(l1, l2)


def merged(scores, virtual, found, values, virtual_values):
    ends = jnp.where(iota((128, 128), 0) == iota((128, 128), 1), virtual, 0.0)
    ends = jnp.sum(ends, axis=0, keepdims=True)
    coarse = jnp.where(found, ends, GONE)
    highest = jnp.maximum(
        jnp.max(scores, axis=1, keepdims=True), jnp.max(coarse, axis=1, keepdims=True)
    )
    weights = jnp.exp2(scores - highest).astype(BF)
    coarse_weights = jnp.exp2(coarse - highest).astype(BF)
    both = dot(
        jnp.concatenate([weights, coarse_weights], 1),
        with_ones(jnp.concatenate([values, virtual_values], 0)),
    )
    return both[:, :DH], both[:, DH:], highest


def fine_kernel(
    edge, qkv, l3, l4, q5, q6, q7, got_a, got_b, got_c, got_d, got_e, o1, e1, o2, e2,
    out, squares, o3, e3, kv,
):
    step = pl.program_id(0)
    zero_tail = jnp.zeros((8, DH), BF)
    odd = edge[0] == 1

    @pl.when(step == 0)
    def _():
        kv[128 : 128 + TOKENS, :] = qkv[:, 256:]

        @pl.when(odd)
        def _():
            kv[:128, :] = got_a[:128, :]
            kv[128 + TOKENS :, :] = got_b[...]

        @pl.when(jnp.logical_not(odd))
        def _():
            kv[:128, :] = got_b[...]
            kv[128 + TOKENS :, :] = got_a[:128, :]

        found = level_matches(128, 4, (4, 5, 6, 7), 1)
        for head in range(HEADS):
            q, k, v = (slice(i * 256 + head * 128, i * 256 + head * 128 + 128) for i in range(3))
            c = slice(head * 128, head * 128 + 128)
            gk, gv = c, slice(256 + head * 128, 256 + head * 128 + 128)
            o4, e4 = [], []
            for block in range(2):
                mine = slice(block * 128, block * 128 + 128)
                its = slice((block ^ 1) * 128, (block ^ 1) * 128 + 128)
                o, e = attend(l4[mine, q], l4[its, k], l4[its, v])
                o4 += [o[:64], o[64:]]
                e4 += [e[:64], e[64:]]
            o5, e5 = attend(q5[:, c], got_a[128:256, gk], got_a[128:256, gv])
            o6, e6 = attend(q6[:, c], got_c[:, gk], got_c[:, gv])
            far = jnp.concatenate([got_d[...], got_e[...]], 0)
            o7, e7 = attend(q7[:, c].astype(BF), far[:, gk], far[:, gv])
            for run in range(4):
                its = slice((run ^ 1) * 128, (run ^ 1) * 128 + 128)
                mine = slice(run * 128, run * 128 + 128)
                virtual_values = jnp.concatenate(
                    [
                        o4[run].astype(F32),
                        o5[run * 32 : run * 32 + 32].astype(F32),
                        o6[run * 16 : run * 16 + 16].astype(F32),
                        o7.astype(F32)[run * 8 : run * 8 + 8],
                        jnp.zeros((8, DH), F32),
                    ],
                    0,
                ).astype(BF)
                virtual = jnp.concatenate(
                    [
                        e4[run],
                        e5[run * 32 : run * 32 + 32],
                        e6[run * 16 : run * 16 + 16],
                        e7[run * 8 : run * 8 + 8],
                        jnp.zeros((8, DH), F32),
                    ],
                    0,
                )
                scores = dot_t(l3[mine, q], l3[its, k]) * SCALE
                weighted, total, highest = merged(scores, virtual, found, l3[its, v], virtual_values)
                o3[mine, c] = (weighted / total).astype(BF)
                e3[mine, c] = highest + jnp.log2(total)

    found = level_matches(128, 1, (1, 2, 3), 1)
    first = jnp.where((step == 0) & (edge[1] == 1), GONE, 0.0)
    last = jnp.where((step == TOKENS // TM - 1) & (edge[2] == 1), GONE, 0.0)
    row = iota((8, 128), 0)
    gathered = jnp.zeros((8, 128), F32)
    for block in range(8):
        at = pl.multiple_of(step * TM + block * 128, 128)
        sums = jnp.zeros((128, DH), F32)
        for head in range(HEADS):
            c = slice(head * 128, head * 128 + 128)
            gk, gv = c, slice(256 + head * 128, 256 + head * 128 + 128)
            scores = dot_t(qkv[pl.ds(at, 128), c], kv[pl.ds(at, 384), gk]) * SCALE
            if block == 0:
                scores = scores + jnp.where(iota((1, 384), 1) < 128, first, 0.0)
            if block == 7:
                scores = scores + jnp.where(iota((1, 384), 1) >= 256, last, 0.0)
            b = step * 8 + block
            at1 = pl.ds(pl.multiple_of(b * 64, 64), 64)
            at2 = pl.ds(pl.multiple_of(b * 32, 32), 32)
            at3 = pl.ds(pl.multiple_of(b * 16, 16), 16)
            virtual_values = jnp.concatenate(
                [o1[at1, c], o2[at2, c], o3[at3, c], jnp.zeros((16, DH), BF)], 0
            )
            virtual = jnp.concatenate(
                [e1[at1, c], e2[at2, c], e3[at3, c], jnp.zeros((16, DH), F32)], 0
            )
            weighted, total, _ = merged(scores, virtual, found, kv[pl.ds(at, 384), gv], virtual_values)
            attention = weighted / total
            out[block * 128 : block * 128 + 128, c] = attention
            sums = sums + attention * attention
        token_sums = dot_t(jnp.ones((8, DH), F32), sums)
        gathered = jnp.where(row == block, token_sums, gathered)
    squares[...] = gathered


def fine(edge, *arrays):
    whole = lambda a: pl.BlockSpec(a.shape, lambda i, p: (0,) * a.ndim)
    tiles = lambda rows, cols: pl.BlockSpec((rows, cols), lambda i, p: (i, 0))
    shape = jax.ShapeDtypeStruct
    return pl.pallas_call(
        fine_kernel,
        grid_spec=pltpu.PrefetchScalarGridSpec(
            num_scalar_prefetch=1,
            grid=(TOKENS // TM,),
            in_specs=[whole(a) for a in arrays],
            out_specs=[tiles(TM, 256), tiles(8, 128)],
            scratch_shapes=[
                pltpu.VMEM((512, 256), BF),
                pltpu.VMEM((512, 256), F32),
                pltpu.VMEM((TOKENS + 256, 512), BF),
            ],
        ),
        out_shape=[shape((TOKENS, 256), F32), shape((32, 128), F32)],
        compiler_params=pltpu.CompilerParams(vmem_limit_bytes=56 * 2**20),
        name="merge_levels",
        cost_estimate=pl.CostEstimate(
            flops=4 * TOKENS * 512 * 256, bytes_accessed=18 * 2**20, transcendentals=TOKENS * 1024
        ),
    )(edge, *arrays)


def norm_kernel(attention, s0, s1, s2, s3, gain, out):
    total = s0[...] + s1[...] + s2[...] + s3[...]
    factor = lax.rsqrt(total / D + 1e-6)
    eye = iota((128, 128), 0) == iota((128, 128), 1)
    for block in range(8):
        mine = slice(block * 128, block * 128 + 128)
        column = jnp.sum(jnp.where(eye, factor[block : block + 1], 0.0), axis=1, keepdims=True)
        out[mine, :] = (attention[mine, :] * column * gain[...]).astype(BF)


def norm(attention, sums, gain):
    tiles = lambda rows, cols: pl.BlockSpec((rows, cols), lambda i: (i, 0))
    return pl.pallas_call(
        norm_kernel,
        grid=(TOKENS // TM,),
        in_specs=[tiles(TM, 256)] + [tiles(8, 128)] * 4 + [pl.BlockSpec((1, 256), lambda i: (0, 0))],
        out_specs=tiles(TM, 256),
        out_shape=jax.ShapeDtypeStruct((TOKENS, 256), BF),
        name="norm",
    )(attention, *sums, gain)


def shards(hidden_states, w_query, w_key, w_value, norm_gain):
    position = lax.axis_index("seq")
    core = lax.axis_index("head") % 2
    x, z = position // SIDE, position % SIDE
    w_mine = jnp.concatenate([w_query, w_key, w_value], axis=1)
    line = jnp.stack([w_mine] + [along_line(w_mine, True, s) for s in SHIFTS])
    pieces = [line] + [along_line(line, False, s) for s in SHIFTS]
    back = jnp.array((0,) + SHIFTS, jnp.int32)
    near_x = jnp.where(core == 0, (x - back[:, None]) % SIDE, (x - back[None, :]) % SIDE)
    near_z = jnp.where(core == 0, (z - back[None, :]) % SIDE, (z - back[:, None]) % SIDE)
    place = jnp.concatenate([(near_x * SIDE + near_z).reshape(16), (position % 2).reshape(1)])
    qkv, l1, l2, l3, l4, q5, q6, q7, send_a, send_b = project(place.astype(jnp.int32), hidden_states, pieces)
    got_a = flipped(send_a, 1)
    got_b = other_side(send_b)
    pair_6 = jnp.concatenate([send_a[256:320], got_a[256:320]], 0)
    pair_7 = jnp.concatenate([send_a[320:352], got_a[320:352]], 0)
    got_c = flipped(pair_6, 2)
    got_d = flipped(pair_7, 4)
    got_e = flipped(pair_7, 6)
    o1, e1, o2, e2 = pairs(l1, l2)
    edge = jnp.stack([position % 2, position == 0, position == 15]).astype(jnp.int32)
    attention, squares = fine(
        edge, qkv, l3, l4, q5, q6, q7, got_a, got_b, got_c, got_d, got_e, o1, e1, o2, e2
    )
    chip = squares + over_heads(squares, lambda i: i ^ 1)
    sums = [chip] + [over_heads(chip, lambda i, s=s: (i + 2 * s) % 8) for s in SHIFTS]
    return norm(attention, sums, norm_gain.reshape(1, 256))


def solution(mesh):
    in_specs = (P("seq", None), P("seq", "head"), P("seq", "head"), P("seq", "head"), P("head"))
    return jax.shard_map(
        shards, mesh=mesh, in_specs=in_specs, out_specs=P("seq", "head"), check_vma=False
    )
```

```python
import jax
import jax.numpy as jnp
import numpy as np
from jax import lax
from jax.experimental import pallas as pl
from jax.experimental.pallas import tpu as pltpu
from jax.sharding import PartitionSpec as P

H = 16
DH = 128
B = 128
D = 2048
HEADS = 2
SIDE = 4
TOKENS = 4096
SCALE = float(DH**-0.5 * np.log2(np.e))
GONE = -1e30
SHIFTS = (1, 3, 2)
BF = jnp.bfloat16
F32 = jnp.float32
TM = 1024
CHUNK = 512
CHUNKS = TOKENS // CHUNK
RUNS = TOKENS // TM
GROUP = 8


def line_perm(first, shift):
    pairs = []
    for x in range(SIDE):
        for z in range(SIDE):
            for head in range(8):
                if (head % 2 == 0) == first:
                    target = x * SIDE + (z + shift) % SIDE
                else:
                    target = (x + shift) % SIDE * SIDE + z
                pairs.append(((x * SIDE + z) * 8 + head, target * 8 + head))
    return pairs


def along_line(value, first, shift):
    return lax.ppermute(value, ("seq", "head"), line_perm(first, shift))


def flipped(value, bits):
    return lax.ppermute(value, "seq", [(i, i ^ bits) for i in range(16)])


def other_side(value):
    pairs = [(i, i + 1) for i in range(1, 15, 2)] + [(i + 1, i) for i in range(1, 15, 2)]
    return lax.ppermute(value, "seq", pairs)


def over_heads(value, step):
    return lax.ppermute(value, "head", [(i, step(i)) for i in range(8)])


def dot(a, b):
    return lax.dot_general(a, b, (((1,), (0,)), ((), ())), preferred_element_type=F32)


def dot_t(a, b):
    return lax.dot_general(a, b, (((1,), (1,)), ((), ())), preferred_element_type=F32)


def iota(shape, dim):
    return lax.broadcasted_iota(jnp.int32, shape, dim)


def level_matches(rows, first, levels, row_dim):
    shape = (128, rows) if row_dim == 1 else (rows, rows)
    token, slot = iota(shape, 0), iota(shape, 1)
    found = jnp.zeros(shape, jnp.bool_)
    start = 0
    for level in levels:
        count = 128 >> (level - first + 1)
        found = found | ((slot - start) == (token >> (level - first + 1)))  & (slot >= start) & (
            slot < start + count
        )
        start += count
    return found


def pool_matrix(rows, tokens, levels, first=0):
    row, token = iota((rows, tokens), 0), iota((rows, tokens), 1)
    total = jnp.zeros((rows, tokens), F32)
    start = 0
    for level in levels:
        count = tokens >> (level - first)
        inside = (row >= start) & (row < start + count) & ((row - start) == (token >> (level - first)))
        total = jnp.where(inside, 2.0 ** (first - level), total)
        start += count
    return total.astype(BF)


def parts_of(source, target, sems, count):
    rows = source.shape[0] // count
    return [
        pltpu.make_async_copy(
            source.at[pl.ds(i * rows, rows)], target.at[pl.ds(i * rows, rows)], sems.at[i]
        )
        for i in range(count)
    ]


def part_of(source, target, sems, index, rows):
    at = pl.ds(pl.multiple_of(index * rows, rows), rows)
    return pltpu.make_async_copy(source.at[at], target.at[at], sems.at[index])


def start_all(copies):
    for copy in copies:
        copy.start()


def wait_all(copies):
    for copy in copies:
        copy.wait()


def moves(pairs, sems):
    return [pltpu.make_async_copy(a, b, sems.at[n]) for n, (a, b) in enumerate(pairs)]


def start_projection(place, hidden, pieces, h_all, w_all, h_sem, w_sem):
    for outer, piece in enumerate(pieces):
        for inner in range(SIDE):
            slot = outer * SIDE + inner
            at = pl.multiple_of(place[slot] * 128, 128)
            pltpu.make_async_copy(piece.at[inner], w_all.at[pl.ds(at, 128)], w_sem.at[slot]).start()
    for index in range(2):
        part_of(hidden, h_all, h_sem, index, CHUNK).start()


def wait_weights(pieces, w_all, w_sem):
    for slot in range(16):
        pltpu.make_async_copy(
            pieces[slot // SIDE].at[slot % SIDE], w_all.at[pl.ds(0, 128)], w_sem.at[slot]
        ).wait()


def next_rows(hidden, h_all, h_sem, index):
    part_of(hidden, h_all, h_sem, index, CHUNK).wait()

    @pl.when(index < CHUNKS - 2)
    def _():
        part_of(hidden, h_all, h_sem, index + 2, CHUNK).start()


def pool_block(p_fine, rows, block, l1, l2, l3):
    pooled = dot(p_fine, rows).astype(BF)
    l1[pl.ds(pl.multiple_of(block * 64, 64), 64), :] = pooled[:64]
    l2[pl.ds(pl.multiple_of(block * 32, 32), 32), :] = pooled[64:96]
    l3[pl.ds(pl.multiple_of(block * 16, 16), 16), :] = pooled[96:112]


def pool_runs(l3):
    p_coarse = pool_matrix(128, 128, (4, 5, 6, 7), 3)
    coarse = [dot(p_coarse, l3[run * 128 : run * 128 + 128, :]) for run in range(4)]
    return [
        jnp.concatenate([c[low:high] for c in coarse], 0).astype(BF)
        for low, high in ((0, 64), (64, 96), (96, 112), (112, 120))
    ]


def keys_kernel(
    place, hidden, w0, w1, w2, w3,
    full_out, l1_out, l2_out, l3_out, l4_out, a_out, b_out, six_out, seven_out,
    h_all, w_all, full, l1, l2, l3, l4, send_a, send_b, six, seven, h_sem, w_sem, out_sem, last_sem,
):
    pieces = (w0, w1, w2, w3)
    start_projection(place, hidden, pieces, h_all, w_all, h_sem, w_sem)
    p_fine = pool_matrix(112, 128, (1, 2, 3))
    wait_weights(pieces, w_all, w_sem)

    def sends(index):
        made = zip((full, l1, l2, l3), (full_out, l1_out, l2_out, l3_out), (1, 2, 4, 8))
        return [
            part_of(v, out, out_sem.at[n], index, CHUNK // ratio)
            for n, (v, out, ratio) in enumerate(made)
        ]

    @pl.loop(0, CHUNKS)
    def _(index):
        next_rows(hidden, h_all, h_sem, index)
        at = pl.ds(pl.multiple_of(index * CHUNK, CHUNK), CHUNK)
        rows = dot(h_all[at, :], w_all[...]).astype(BF)
        full[at, :] = rows
        for part in range(CHUNK // 128):
            pool_block(p_fine, rows[part * 128 : part * 128 + 128], index * (CHUNK // 128) + part, l1, l2, l3)
        start_all(sends(index))

    l4[...], five, six[...], seven[...] = pool_runs(l3)
    odd = place[16] == 1
    low, high = full[:128, :], full[TOKENS - 128 :, :]
    send_a[:128, :] = jnp.where(odd, low, high)
    send_b[...] = jnp.where(odd, high, low)
    send_a[128:, :] = five
    pairs = ((l4, l4_out), (send_a, a_out), (send_b, b_out), (six, six_out), (seven, seven_out))
    last = moves(pairs, last_sem)
    start_all(last)

    @pl.loop(0, CHUNKS)
    def _(index):
        wait_all(sends(index))

    wait_all(last)


def queries_kernel(
    place, hidden, w0, w1, w2, w3, kv1, kv2,
    full_out, o1_out, o2_out, virtual_out, q3_out, q4_out, q5_out, q6_out, q7_out,
    h_all, w_all, full, l1, l2, l3, q4, q5, q6, q7, kv1_all, kv2_all, o1, o2, virtual,
    h_sem, w_sem, kv_sem, out_sem, last_sem,
):
    pieces = (w0, w1, w2, w3)
    start_projection(place, hidden, pieces, h_all, w_all, h_sem, w_sem)
    p_fine = pool_matrix(112, 128, (1, 2, 3))
    wait_weights(pieces, w_all, w_sem)
    arriving = [parts_of(kv1, kv1_all, kv_sem.at[0], RUNS), parts_of(kv2, kv2_all, kv_sem.at[1], RUNS)]
    leaving = [
        parts_of(mine, out, out_sem.at[n], RUNS)
        for n, (mine, out) in enumerate(((full, full_out), (o1, o1_out), (o2, o2_out)))
    ]

    def attend_run(run):
        wait_all([group[run] for group in arriving])
        triples, places = [], []
        for head in range(HEADS):
            k, v = (slice(i * 256 + head * 128, i * 256 + head * 128 + 128) for i in range(2))
            for q_all, kv_all, out, count in ((l1, kv1_all, o1, 4), (l2, kv2_all, o2, 2)):
                for block in range(run * count, run * count + count):
                    mine = slice(block * 128, block * 128 + 128)
                    its = slice((block ^ 1) * 128, (block ^ 1) * 128 + 128)
                    triples.append((q_all[mine, k], kv_all[its, k], kv_all[its, v]))
                    places.append((out, mine, k))
        done = attend_all(triples)
        for (out, mine, k), (rows, _) in zip(places, done):
            out[mine, k] = rows
        for head in range(HEADS):
            ends = [level_row(total) for _, total in done[head * 6 : head * 6 + 6]]
            lanes = []
            for block in range(8):
                fine = ends[block // 2][:, block % 2 * 64 : block % 2 * 64 + 64]
                coarse = ends[4 + block // 4][:, block % 4 * 32 : block % 4 * 32 + 32]
                lanes.append(jnp.concatenate([fine, coarse, jnp.zeros((1, 32), F32)], 1))
            virtual[run * 8 : run * 8 + 8, head * 128 : head * 128 + 128] = jnp.concatenate(lanes, 0)

    for run in range(RUNS):
        for index in range(run * (TM // CHUNK), (run + 1) * (TM // CHUNK)):
            next_rows(hidden, h_all, h_sem, jnp.int32(index))
        start_all([group[run] for group in arriving])
        at = slice(run * TM, run * TM + TM)
        rows = (dot(h_all[at, :], w_all[...]) * SCALE).astype(BF)
        full[at, :] = rows
        leaving[0][run].start()
        for part in range(TM // 128):
            pool_block(p_fine, rows[part * 128 : part * 128 + 128], run * (TM // 128) + part, l1, l2, l3)
        if run:
            attend_run(run - 1)
            leaving[1][run - 1].start()
            leaving[2][run - 1].start()
    q4[...], q5[...], q6[...], q7[...] = pool_runs(l3)
    attend_run(RUNS - 1)
    leaving[1][RUNS - 1].start()
    leaving[2][RUNS - 1].start()
    pairs = ((virtual, virtual_out), (l3, q3_out), (q4, q4_out), (q5, q5_out), (q6, q6_out), (q7, q7_out))
    last = moves(pairs, last_sem)
    start_all(last)
    for group in leaving:
        wait_all(group)
    wait_all(last)


def project_keys(place, hidden, pieces):
    anywhere = pl.BlockSpec(memory_space=pl.ANY)
    levels = [(TOKENS >> level, 512) for level in range(5)]
    small = [(256, 512), (128, 512), (64, 512), (32, 512)]
    return pl.pallas_call(
        keys_kernel,
        in_specs=[pl.BlockSpec(memory_space=pltpu.SMEM)] + [anywhere] * 5,
        out_specs=[anywhere] * 9,
        out_shape=[jax.ShapeDtypeStruct(size, BF) for size in levels + small],
        scratch_shapes=[
            pltpu.VMEM((TOKENS, D), BF),
            pltpu.VMEM((D, 512), BF),
            *[pltpu.VMEM(size, BF) for size in levels + small],
            pltpu.SemaphoreType.DMA((CHUNKS,)),
            pltpu.SemaphoreType.DMA((16,)),
            pltpu.SemaphoreType.DMA((4, CHUNKS)),
            pltpu.SemaphoreType.DMA((5,)),
        ],
        compiler_params=pltpu.CompilerParams(vmem_limit_bytes=56 * 2**20),
        name="project_keys",
        cost_estimate=pl.CostEstimate(
            flops=2 * TOKENS * D * 512, bytes_accessed=26 * 2**20, transcendentals=0
        ),
    )(place, hidden, *pieces)


def project_queries(place, hidden, pieces, kv1, kv2):
    anywhere = pl.BlockSpec(memory_space=pl.ANY)
    shape = jax.ShapeDtypeStruct
    small = [shape((size, 256), BF) for size in (512, 256, 128, 64, 32)]
    buffer = lambda *size: pltpu.VMEM(size, BF)
    return pl.pallas_call(
        queries_kernel,
        in_specs=[pl.BlockSpec(memory_space=pltpu.SMEM)] + [anywhere] * 7,
        out_specs=[anywhere] * 9,
        out_shape=[shape((TOKENS, 256), BF), shape((2048, 256), BF), shape((1024, 256), BF)]
        + [shape((32, 256), F32)]
        + small,
        scratch_shapes=[
            buffer(TOKENS, D),
            buffer(D, 256),
            *[buffer(TOKENS >> level, 256) for level in range(4)],
            *[buffer(size, 256) for size in (256, 128, 64, 32)],
            buffer(2048, 512),
            buffer(1024, 512),
            buffer(2048, 256),
            buffer(1024, 256),
            pltpu.VMEM((32, 256), F32),
            pltpu.SemaphoreType.DMA((CHUNKS,)),
            pltpu.SemaphoreType.DMA((16,)),
            pltpu.SemaphoreType.DMA((2, RUNS)),
            pltpu.SemaphoreType.DMA((3, RUNS)),
            pltpu.SemaphoreType.DMA((6,)),
        ],
        compiler_params=pltpu.CompilerParams(vmem_limit_bytes=56 * 2**20),
        name="project_queries",
        cost_estimate=pl.CostEstimate(
            flops=2 * TOKENS * D * 256, bytes_accessed=26 * 2**20, transcendentals=2**20
        ),
    )(place, hidden, *pieces, kv1, kv2)


def with_ones(values):
    return jnp.concatenate([values, jnp.ones_like(values)], axis=1)


def quotient(rows, total):
    inverse = pl.reciprocal(total, approx=True)
    return rows * (inverse * (2.0 - total * inverse))


def attend_all(triples):
    scores = [dot_t(queries, key_rows) for queries, key_rows, _ in triples]
    highest = [jnp.max(s, axis=1, keepdims=True) for s in scores]
    weights = [jnp.exp2(s - h).astype(BF) for s, h in zip(scores, highest)]
    both = [dot(w, with_ones(values)) for w, (_, _, values) in zip(weights, triples)]
    return [
        (quotient(o[:, :DH], o[:, DH:]).astype(BF), h + jnp.log2(o[:, DH:])) for o, h in zip(both, highest)
    ]


def level_row(total):
    eye = iota((128, 128), 0) == iota((128, 128), 1)
    return jnp.sum(jnp.where(eye, total, 0.0), axis=0, keepdims=True)


def merged(parts, found):
    scores = [dot_t(queries, key_rows) for queries, key_rows, *_ in parts]
    scores = [s if p[5] is None else s + p[5] for s, p in zip(scores, parts)]
    coarse = [jnp.where(found, p[3], GONE) for p in parts]
    highest = [
        jnp.maximum(jnp.max(s, axis=1, keepdims=True), jnp.max(c, axis=1, keepdims=True))
        for s, c in zip(scores, coarse)
    ]
    weights = [
        jnp.concatenate([jnp.exp2(s - h).astype(BF), jnp.exp2(c - h).astype(BF)], 1)
        for s, c, h in zip(scores, coarse, highest)
    ]
    both = [
        dot(w, with_ones(jnp.concatenate([p[2], p[4]], 0))) for w, p in zip(weights, parts)
    ]
    return [(o[:, :DH], o[:, DH:], h) for o, h in zip(both, highest)]


def fine_kernel(
    edge, q3_in, kv3_in, q4_in, kv4_in, q5_in, q6_in, q7_in, got_a, got_b, got_d, got_s, got_c, got_e,
    virtual_in, q, kv, o1, o2, out, squares,
    q3, kv3, q4, kv4, q5, q6, q7, kv5, kv6, kv7, virtual,
    q_all, kv_all, o1_all, o2_all, o3, virtual_3, out_all, first_sem, in_sem, out_sem,
):
    odd = edge[0] == 1
    above, below = 0, 128 + TOKENS
    at_a = pl.ds(pl.multiple_of(jnp.where(odd, above, below), 128), 128)
    at_b = pl.ds(pl.multiple_of(jnp.where(odd, below, above), 128), 128)
    early = moves(
        (
            (q4_in, q4),
            (kv4_in, kv4),
            (q5_in, q5),
            (q6_in, q6),
            (q7_in, q7),
            (got_a.at[pl.ds(128, 128)], kv5),
            (got_c.at[pl.ds(0, 64)], kv6.at[pl.ds(0, 64)]),
            (got_e.at[pl.ds(0, 64)], kv6.at[pl.ds(64, 64)]),
            (got_d, kv7.at[pl.ds(0, 32)]),
            (got_s, kv7.at[pl.ds(32, 32)]),
            (got_c.at[pl.ds(64, 32)], kv7.at[pl.ds(64, 32)]),
            (got_e.at[pl.ds(64, 32)], kv7.at[pl.ds(96, 32)]),
            (q3_in, q3),
            (kv3_in, kv3),
            (virtual_in, virtual),
            (got_a.at[pl.ds(0, 128)], kv_all.at[at_a]),
            (got_b, kv_all.at[at_b]),
        ),
        first_sem,
    )
    inner = kv_all.at[pl.ds(128, TOKENS)]
    groups = ((q, q_all), (kv, inner), (o1, o1_all), (o2, o2_all))
    arriving = [parts_of(a, b, in_sem.at[n], RUNS) for n, (a, b) in enumerate(groups)]
    start_all(early)
    for part in range(2):
        start_all([group[part] for group in arriving])
    wait_all(early)

    found = level_matches(128, 4, (4, 5, 6, 7), 1)
    triples = []
    for head in range(HEADS):
        k, v = (slice(i * 256 + head * 128, i * 256 + head * 128 + 128) for i in range(2))
        for block in range(2):
            mine = slice(block * 128, block * 128 + 128)
            its = slice((block ^ 1) * 128, (block ^ 1) * 128 + 128)
            triples.append((q4[mine, k], kv4[its, k], kv4[its, v]))
        triples.append((q5[:, k], kv5[:, k], kv5[:, v]))
        triples.append((q6[:, k], kv6[:, k], kv6[:, v]))
        triples.append((q7[:, k], kv7[:, k], kv7[:, v]))
    done = attend_all(triples)
    parts = []
    for head in range(HEADS):
        k, v = (slice(i * 256 + head * 128, i * 256 + head * 128 + 128) for i in range(2))
        (oa, ea), (ob, eb), (o5, e5), (o6, e6), (o7, e7) = done[head * 5 : head * 5 + 5]
        for run in range(4):
            its = slice((run ^ 1) * 128, (run ^ 1) * 128 + 128)
            mine = slice(run * 128, run * 128 + 128)
            half = slice(run % 2 * 64, run % 2 * 64 + 64)
            values = jnp.concatenate(
                [
                    (oa, ob)[run // 2][half].astype(F32),
                    o5[run * 32 : run * 32 + 32].astype(F32),
                    o6[run * 16 : run * 16 + 16].astype(F32),
                    o7.astype(F32)[run * 8 : run * 8 + 8],
                    jnp.zeros((8, DH), F32),
                ],
                0,
            ).astype(BF)
            total = jnp.concatenate(
                [
                    (ea, eb)[run // 2][half],
                    e5[run * 32 : run * 32 + 32],
                    e6[run * 16 : run * 16 + 16],
                    e7[run * 8 : run * 8 + 8],
                    jnp.zeros((8, DH), F32),
                ],
                0,
            )
            parts.append((q3[mine, k], kv3[its, k], kv3[its, v], level_row(total), values, None))
    for index, (weighted, total, highest) in enumerate(merged(parts, found)):
        head, run = divmod(index, 4)
        c = slice(head * 128, head * 128 + 128)
        o3[run * 128 : run * 128 + 128, c] = quotient(weighted, total).astype(BF)
        ends = level_row(highest + jnp.log2(total))
        lanes = [
            jnp.concatenate(
                [jnp.zeros((1, 96), F32), ends[:, block * 16 : block * 16 + 16], jnp.zeros((1, 16), F32)], 1
            )
            for block in range(8)
        ]
        mine = slice(run * 8, run * 8 + 8)
        virtual_3[mine, c] = jnp.concatenate(lanes, 0) + virtual[mine, c]

    found = level_matches(128, 1, (1, 2, 3), 1)
    row = iota((8, 128), 0)
    arriving[1][0].wait()

    @pl.loop(0, RUNS)
    def _(step):
        part_of(q, q_all, in_sem.at[0], step, TM).wait()
        part_of(o1, o1_all, in_sem.at[2], step, TM // 2).wait()
        part_of(o2, o2_all, in_sem.at[3], step, TM // 4).wait()

        @pl.when(step < RUNS - 2)
        def _():
            part_of(q, q_all, in_sem.at[0], step + 2, TM).start()
            part_of(kv, inner, in_sem.at[1], step + 2, TM).start()
            part_of(o1, o1_all, in_sem.at[2], step + 2, TM // 2).start()
            part_of(o2, o2_all, in_sem.at[3], step + 2, TM // 4).start()

        @pl.when(step < RUNS - 1)
        def _():
            part_of(kv, inner, in_sem.at[1], step + 1, TM).wait()

        first = jnp.where((step == 0) & (edge[1] == 1), GONE, 0.0)
        last = jnp.where((step == 3) & (edge[2] == 1), GONE, 0.0)
        gathered = jnp.zeros((8, 128), F32)
        levels = virtual_3[pl.ds(pl.multiple_of(step * 8, 8), 8), :]
        for group in range(8 // GROUP):
            parts = []
            for block in range(group * GROUP, group * GROUP + GROUP):
                at = pl.multiple_of(step * TM + block * 128, 128)
                b = step * 8 + block
                at1 = pl.ds(pl.multiple_of(b * 64, 64), 64)
                at2 = pl.ds(pl.multiple_of(b * 32, 32), 32)
                at3 = pl.ds(pl.multiple_of(b * 16, 16), 16)
                bias = None
                if block == 0:
                    bias = jnp.where(iota((1, 384), 1) < 128, first, 0.0)
                if block == 7:
                    bias = jnp.where(iota((1, 384), 1) >= 256, last, 0.0)
                for head in range(HEADS):
                    c, gv = (slice(i * 256 + head * 128, i * 256 + head * 128 + 128) for i in range(2))
                    values = jnp.concatenate(
                        [o1_all[at1, c], o2_all[at2, c], o3[at3, c], jnp.zeros((16, DH), BF)], 0
                    )
                    parts.append(
                        (
                            q_all[pl.ds(at, 128), c],
                            kv_all[pl.ds(at, 384), c],
                            kv_all[pl.ds(at, 384), gv],
                            levels[block : block + 1, c],
                            values,
                            bias,
                        )
                    )
            done = merged(parts, found)
            for index, block in enumerate(range(group * GROUP, group * GROUP + GROUP)):
                sums = jnp.zeros((128, DH), F32)
                at = pl.ds(pl.multiple_of(step * TM + block * 128, 128), 128)
                for head in range(HEADS):
                    weighted, total, _ = done[index * HEADS + head]
                    attention = quotient(weighted, total)
                    out_all[at, head * 128 : head * 128 + 128] = attention.astype(BF)
                    sums = sums + attention * attention
                token_sums = dot_t(jnp.ones((8, DH), F32), sums)
                gathered = jnp.where(row == block, token_sums, gathered)
        squares[pl.ds(pl.multiple_of(step * 8, 8), 8), :] = gathered
        part_of(out_all, out, out_sem, step, TM).start()

    @pl.loop(0, 4)
    def _(step):
        part_of(out_all, out, out_sem, step, TM).wait()


def fine(edge, *arrays):
    anywhere = pl.BlockSpec(memory_space=pl.ANY)
    local = pl.BlockSpec(memory_space=pltpu.VMEM)
    shape = jax.ShapeDtypeStruct
    buffer = lambda *size: pltpu.VMEM(size, BF)
    return pl.pallas_call(
        fine_kernel,
        in_specs=[pl.BlockSpec(memory_space=pltpu.SMEM)] + [anywhere] * len(arrays),
        out_specs=[anywhere, local],
        scratch_shapes=[
            buffer(512, 256),
            buffer(512, 512),
            buffer(256, 256),
            buffer(256, 512),
            *[buffer(size, 256) for size in (128, 64, 32)],
            *[buffer(128, 512)] * 3,
            pltpu.VMEM((32, 256), F32),
            buffer(TOKENS, 256),
            buffer(TOKENS + 256, 512),
            buffer(TOKENS // 2, 256),
            buffer(TOKENS // 4, 256),
            buffer(512, 256),
            pltpu.VMEM((32, 256), F32),
            buffer(TOKENS, 256),
            pltpu.SemaphoreType.DMA((17,)),
            pltpu.SemaphoreType.DMA((4, RUNS)),
            pltpu.SemaphoreType.DMA((RUNS,)),
        ],
        out_shape=[shape((TOKENS, 256), BF), shape((32, 128), F32)],
        compiler_params=pltpu.CompilerParams(vmem_limit_bytes=56 * 2**20),
        name="merge_levels",
        cost_estimate=pl.CostEstimate(
            flops=4 * TOKENS * 512 * 256, bytes_accessed=18 * 2**20, transcendentals=TOKENS * 1024
        ),
    )(edge, *arrays)


def norm_kernel(attention, s0, s1, s2, s3, gain, out, rows, done, in_sem, out_sem):
    arriving = parts_of(attention, rows, in_sem, 4)
    leaving = parts_of(done, out, out_sem, 4)
    start_all(arriving)
    total = s0[...] + s1[...] + s2[...] + s3[...]
    factor = lax.rsqrt(total / D + 1e-6)
    eye = iota((128, 128), 0) == iota((128, 128), 1)
    for part in range(4):
        arriving[part].wait()
        for block in range(part * 8, part * 8 + 8):
            mine = slice(block * 128, block * 128 + 128)
            column = jnp.sum(jnp.where(eye, factor[block : block + 1], 0.0), axis=1, keepdims=True)
            done[mine, :] = (rows[mine, :].astype(F32) * column * gain[...]).astype(BF)
        leaving[part].start()
    wait_all(leaving)


def norm(attention, sums, gain):
    anywhere = pl.BlockSpec(memory_space=pl.ANY)
    local = pl.BlockSpec(memory_space=pltpu.VMEM)
    return pl.pallas_call(
        norm_kernel,
        in_specs=[anywhere] + [local] * 5,
        out_specs=anywhere,
        out_shape=jax.ShapeDtypeStruct((TOKENS, 256), BF),
        scratch_shapes=[
            pltpu.VMEM((TOKENS, 256), BF),
            pltpu.VMEM((TOKENS, 256), BF),
            pltpu.SemaphoreType.DMA((4,)),
            pltpu.SemaphoreType.DMA((4,)),
        ],
        compiler_params=pltpu.CompilerParams(vmem_limit_bytes=56 * 2**20),
        name="norm",
    )(attention, *sums, gain)


def join_kernel(a, b, c, out):
    out[:, :256] = a[...]
    out[:, 256:512] = b[...]
    out[:, 512:] = c[...]


def joined(*weights):
    local = pl.BlockSpec(memory_space=pltpu.VMEM)
    return pl.pallas_call(
        join_kernel,
        in_specs=[local] * 3,
        out_specs=local,
        out_shape=jax.ShapeDtypeStruct((128, 768), BF),
        name="join_weights",
    )(*weights)


def shards(hidden_states, w_query, w_key, w_value, norm_gain):
    position = lax.axis_index("seq")
    core = lax.axis_index("head") % 2
    x, z = position // SIDE, position % SIDE
    w_mine = joined(w_key, w_value, w_query)
    line = jnp.stack([w_mine] + [along_line(w_mine, True, s) for s in SHIFTS])
    line_kv, line_q = line[:, :, :512], line[:, :, 512:]
    pieces_kv = [line_kv] + [along_line(line_kv, False, s) for s in SHIFTS]
    pieces_q = [line_q] + [along_line(line_q, False, s) for s in SHIFTS]
    back = jnp.array((0,) + SHIFTS, jnp.int32)
    near_x = jnp.where(core == 0, (x - back[:, None]) % SIDE, (x - back[None, :]) % SIDE)
    near_z = jnp.where(core == 0, (z - back[None, :]) % SIDE, (z - back[:, None]) % SIDE)
    place = jnp.concatenate([(near_x * SIDE + near_z).reshape(16), (position % 2).reshape(1)])
    place = place.astype(jnp.int32)
    kv, kv1, kv2, kv3, kv4, send_a, send_b, send_6, send_7 = project_keys(place, hidden_states, pieces_kv)
    got_d = flipped(send_7, 4)
    got_a = flipped(send_a, 1)
    got_b = other_side(send_b)
    far = jnp.concatenate([send_6, got_d], 0)
    got_s = flipped(got_d, 1)
    got_c = flipped(far, 2)
    got_e = flipped(far, 3)
    q, o1, o2, virtual, q3, q4, q5, q6, q7 = project_queries(place, hidden_states, pieces_q, kv1, kv2)
    edge = jnp.stack([position % 2, position == 0, position == 15]).astype(jnp.int32)
    attention, squares = fine(
        edge, q3, kv3, q4, kv4, q5, q6, q7, got_a, got_b, got_d, got_s, got_c, got_e, virtual, q, kv, o1, o2
    )
    chip = squares + over_heads(squares, lambda i: i ^ 1)
    sums = [chip] + [over_heads(chip, lambda i, s=s: (i + 2 * s) % 8) for s in SHIFTS]
    return norm(attention, sums, norm_gain.reshape(1, 256))


def solution(mesh):
    in_specs = (P("seq", None), P("seq", "head"), P("seq", "head"), P("seq", "head"), P("head"))
    return jax.shard_map(
        shards, mesh=mesh, in_specs=in_specs, out_specs=P("seq", "head"), check_vma=False
    )
```

```python
import jax
import jax.numpy as jnp
import numpy as np
from jax import lax
from jax.experimental import pallas as pl
from jax.experimental.pallas import tpu as pltpu
from jax.sharding import PartitionSpec as P

H = 16
DH = 128
B = 128
D = 2048
HEADS = 2
SIDE = 4
TOKENS = 4096
SCALE = float(DH**-0.5 * np.log2(np.e))
GONE = -1e30
SHIFTS = (1, 3, 2)
BF = jnp.bfloat16
F32 = jnp.float32
TM = 1024
CHUNK = 512
CHUNKS = TOKENS // CHUNK
RUNS = TOKENS // TM
VMEM_LIMIT = 32 * 2**20
GROUP = 8


def line_perm(first, shift):
    pairs = []
    for x in range(SIDE):
        for z in range(SIDE):
            for head in range(8):
                if (head % 2 == 0) == first:
                    target = x * SIDE + (z + shift) % SIDE
                else:
                    target = (x + shift) % SIDE * SIDE + z
                pairs.append(((x * SIDE + z) * 8 + head, target * 8 + head))
    return pairs


def along_line(value, first, shift):
    return lax.ppermute(value, ("seq", "head"), line_perm(first, shift))


def flipped(value, bits):
    return lax.ppermute(value, "seq", [(i, i ^ bits) for i in range(16)])


def other_side(value):
    pairs = [(i, i + 1) for i in range(1, 15, 2)] + [(i + 1, i) for i in range(1, 15, 2)]
    return lax.ppermute(value, "seq", pairs)


def over_heads(value, step):
    return lax.ppermute(value, "head", [(i, step(i)) for i in range(8)])


def dot(a, b):
    return lax.dot_general(a, b, (((1,), (0,)), ((), ())), preferred_element_type=F32)


def dot_t(a, b):
    return lax.dot_general(a, b, (((1,), (1,)), ((), ())), preferred_element_type=F32)


def iota(shape, dim):
    return lax.broadcasted_iota(jnp.int32, shape, dim)


def level_matches(rows, first, levels, row_dim):
    shape = (128, rows) if row_dim == 1 else (rows, rows)
    token, slot = iota(shape, 0), iota(shape, 1)
    found = jnp.zeros(shape, jnp.bool_)
    start = 0
    for level in levels:
        count = 128 >> (level - first + 1)
        found = found | ((slot - start) == (token >> (level - first + 1)))  & (slot >= start) & (
            slot < start + count
        )
        start += count
    return found


def pool_matrix(rows, tokens, levels, first=0):
    row, token = iota((rows, tokens), 0), iota((rows, tokens), 1)
    total = jnp.zeros((rows, tokens), F32)
    start = 0
    for level in levels:
        count = tokens >> (level - first)
        inside = (row >= start) & (row < start + count) & ((row - start) == (token >> (level - first)))
        total = jnp.where(inside, 2.0 ** (first - level), total)
        start += count
    return total.astype(BF)


def parts_of(source, target, sems, count):
    rows = source.shape[0] // count
    return [
        pltpu.make_async_copy(
            source.at[pl.ds(i * rows, rows)], target.at[pl.ds(i * rows, rows)], sems.at[i]
        )
        for i in range(count)
    ]


def part_of(source, target, sems, index, rows):
    at = pl.ds(pl.multiple_of(index * rows, rows), rows)
    return pltpu.make_async_copy(source.at[at], target.at[at], sems.at[index])


def start_all(copies):
    for copy in copies:
        copy.start()


def wait_all(copies):
    for copy in copies:
        copy.wait()


def next_rows(hidden, h_all, h_sem, index):
    part_of(hidden, h_all, h_sem, index, CHUNK).wait()

    @pl.when(index < CHUNKS - 2)
    def _():
        part_of(hidden, h_all, h_sem, index + 2, CHUNK).start()


def place_weights(place, pieces, w_all):
    for outer, piece in enumerate(pieces):
        for inner in range(SIDE):
            at = pl.multiple_of(place[outer * SIDE + inner] * 128, 128)
            w_all[pl.ds(at, 128), :] = piece[inner]


def pool_block(p_fine, rows, block, l1, l2, l3):
    pooled = dot(p_fine, rows).astype(BF)
    l1[pl.ds(pl.multiple_of(block * 64, 64), 64), :] = pooled[:64]
    l2[pl.ds(pl.multiple_of(block * 32, 32), 32), :] = pooled[64:96]
    l3[pl.ds(pl.multiple_of(block * 16, 16), 16), :] = pooled[96:112]


def pool_runs(l3):
    p_coarse = pool_matrix(128, 128, (4, 5, 6, 7), 3)
    coarse = [dot(p_coarse, l3[run * 128 : run * 128 + 128, :]) for run in range(4)]
    return [
        jnp.concatenate([c[low:high] for c in coarse], 0).astype(BF)
        for low, high in ((0, 64), (64, 96), (96, 112), (112, 120))
    ]


def keys_kernel(
    place, hidden, w0, w1, w2, w3, full, l1, l2, l3, l4, send_a, send_b, six, seven, h_all, w_all, h_sem
):
    for index in range(2):
        part_of(hidden, h_all, h_sem, index, CHUNK).start()
    place_weights(place, (w0, w1, w2, w3), w_all)
    p_fine = pool_matrix(112, 128, (1, 2, 3))

    @pl.loop(0, CHUNKS)
    def _(index):
        next_rows(hidden, h_all, h_sem, index)
        at = pl.ds(pl.multiple_of(index * CHUNK, CHUNK), CHUNK)
        rows = dot(h_all[at, :], w_all[...]).astype(BF)
        full[at, :] = rows
        for part in range(CHUNK // 128):
            pool_block(p_fine, rows[part * 128 : part * 128 + 128], index * (CHUNK // 128) + part, l1, l2, l3)

    l4[...], five, six[...], seven[...] = pool_runs(l3)
    odd = place[16] == 1
    low, high = full[:128, :], full[TOKENS - 128 :, :]
    send_a[:128, :] = jnp.where(odd, low, high)
    send_b[...] = jnp.where(odd, high, low)
    send_a[128:, :] = five


def queries_kernel(
    place, hidden, w0, w1, w2, w3, kv1, kv2,
    full, o1, o2, virtual, l3, q4, q5, q6, q7,
    h_all, w_all, l1, l2, h_sem,
):
    for index in range(2):
        part_of(hidden, h_all, h_sem, index, CHUNK).start()
    place_weights(place, (w0, w1, w2, w3), w_all)
    p_fine = pool_matrix(112, 128, (1, 2, 3))

    def attend_run(run):
        triples, places = [], []
        for head in range(HEADS):
            k, v = (slice(i * 256 + head * 128, i * 256 + head * 128 + 128) for i in range(2))
            for q_all, kv_all, out, count in ((l1, kv1, o1, 4), (l2, kv2, o2, 2)):
                for block in range(run * count, run * count + count):
                    mine = slice(block * 128, block * 128 + 128)
                    its = slice((block ^ 1) * 128, (block ^ 1) * 128 + 128)
                    triples.append((q_all[mine, k], kv_all[its, k], kv_all[its, v]))
                    places.append((out, mine, k))
        done = attend_all(triples)
        for (out, mine, k), (rows, _) in zip(places, done):
            out[mine, k] = rows
        for head in range(HEADS):
            ends = [level_row(total) for _, total in done[head * 6 : head * 6 + 6]]
            lanes = []
            for block in range(8):
                fine = ends[block // 2][:, block % 2 * 64 : block % 2 * 64 + 64]
                coarse = ends[4 + block // 4][:, block % 4 * 32 : block % 4 * 32 + 32]
                lanes.append(jnp.concatenate([fine, coarse, jnp.zeros((1, 32), F32)], 1))
            virtual[run * 8 : run * 8 + 8, head * 128 : head * 128 + 128] = jnp.concatenate(lanes, 0)

    for run in range(RUNS):
        for index in range(run * (TM // CHUNK), (run + 1) * (TM // CHUNK)):
            next_rows(hidden, h_all, h_sem, jnp.int32(index))
        at = slice(run * TM, run * TM + TM)
        rows = dot(h_all[at, :], w_all[...]).astype(BF)
        full[at, :] = rows
        for part in range(TM // 128):
            pool_block(p_fine, rows[part * 128 : part * 128 + 128], run * (TM // 128) + part, l1, l2, l3)
        if run:
            attend_run(run - 1)
    q4[...], q5[...], q6[...], q7[...] = pool_runs(l3)
    attend_run(RUNS - 1)


def project_keys(place, hidden, pieces):
    anywhere = pl.BlockSpec(memory_space=pl.ANY)
    local = pl.BlockSpec(memory_space=pltpu.VMEM)
    sizes = [TOKENS >> level for level in range(5)] + [256, 128, 64, 32]
    return pl.pallas_call(
        keys_kernel,
        in_specs=[pl.BlockSpec(memory_space=pltpu.SMEM), anywhere] + [local] * 4,
        out_specs=[local] * 9,
        out_shape=[jax.ShapeDtypeStruct((size, 512), BF) for size in sizes],
        scratch_shapes=[
            pltpu.VMEM((TOKENS, D), BF),
            pltpu.VMEM((D, 512), BF),
            pltpu.SemaphoreType.DMA((CHUNKS,)),
        ],
        compiler_params=pltpu.CompilerParams(vmem_limit_bytes=VMEM_LIMIT),
        name="project_keys",
        cost_estimate=pl.CostEstimate(
            flops=2 * TOKENS * D * 512, bytes_accessed=26 * 2**20, transcendentals=0
        ),
    )(place, hidden, *pieces)


def project_queries(place, hidden, pieces, kv1, kv2):
    anywhere = pl.BlockSpec(memory_space=pl.ANY)
    local = pl.BlockSpec(memory_space=pltpu.VMEM)
    shape = jax.ShapeDtypeStruct
    small = [shape((size, 256), BF) for size in (512, 256, 128, 64, 32)]
    return pl.pallas_call(
        queries_kernel,
        in_specs=[pl.BlockSpec(memory_space=pltpu.SMEM), anywhere] + [local] * 6,
        out_specs=[local] * 9,
        out_shape=[shape((TOKENS, 256), BF), shape((2048, 256), BF), shape((1024, 256), BF)]
        + [shape((32, 256), F32)]
        + small,
        scratch_shapes=[
            pltpu.VMEM((TOKENS, D), BF),
            pltpu.VMEM((D, 256), BF),
            pltpu.VMEM((2048, 256), BF),
            pltpu.VMEM((1024, 256), BF),
            pltpu.SemaphoreType.DMA((CHUNKS,)),
        ],
        compiler_params=pltpu.CompilerParams(vmem_limit_bytes=VMEM_LIMIT),
        name="project_queries",
        cost_estimate=pl.CostEstimate(
            flops=2 * TOKENS * D * 256, bytes_accessed=26 * 2**20, transcendentals=2**20
        ),
    )(place, hidden, *pieces, kv1, kv2)


def with_ones(values):
    return jnp.concatenate([values, jnp.ones_like(values)], axis=1)


def quotient(rows, total):
    inverse = pl.reciprocal(total, approx=True)
    return rows * (inverse * (2.0 - total * inverse))


def attend_all(triples):
    scores = [dot_t(queries, key_rows) * SCALE for queries, key_rows, _ in triples]
    highest = [jnp.max(s, axis=1, keepdims=True) for s in scores]
    weights = [jnp.exp2(s - h).astype(BF) for s, h in zip(scores, highest)]
    both = [dot(w, with_ones(values)) for w, (_, _, values) in zip(weights, triples)]
    return [
        (quotient(o[:, :DH], o[:, DH:]).astype(BF), h + jnp.log2(o[:, DH:])) for o, h in zip(both, highest)
    ]


def level_row(total):
    eye = iota((128, 128), 0) == iota((128, 128), 1)
    return jnp.sum(jnp.where(eye, total, 0.0), axis=0, keepdims=True)


def merged(parts, found):
    scores = [dot_t(queries, key_rows) * SCALE for queries, key_rows, *_ in parts]
    scores = [s if p[5] is None else s + p[5] for s, p in zip(scores, parts)]
    coarse = [jnp.where(found, p[3], GONE) for p in parts]
    highest = [
        jnp.maximum(jnp.max(s, axis=1, keepdims=True), jnp.max(c, axis=1, keepdims=True))
        for s, c in zip(scores, coarse)
    ]
    weights = [
        jnp.concatenate([jnp.exp2(s - h).astype(BF), jnp.exp2(c - h).astype(BF)], 1)
        for s, c, h in zip(scores, coarse, highest)
    ]
    both = [
        dot(w, with_ones(jnp.concatenate([p[2], p[4]], 0))) for w, p in zip(weights, parts)
    ]
    return [(o[:, :DH], o[:, DH:], h) for o, h in zip(both, highest)]


def fine_kernel(
    edge, q3, kv3, q4, kv4, q5, q6, q7, got_a, got_b, got_d, got_s, got_c, got_e, virtual, q, kv, o1, o2,
    out, squares, o3, virtual_3,
):
    odd = edge[0] == 1
    kv5 = got_a.at[pl.ds(128, 128)]
    kv6 = jnp.concatenate([got_c[:64, :], got_e[:64, :]], 0)
    kv7 = jnp.concatenate([got_d[...], got_s[...], got_c[64:, :], got_e[64:, :]], 0)
    above = jnp.where(odd, got_a[:128, :], got_b[...])
    below = jnp.where(odd, got_b[...], got_a[:128, :])
    found = level_matches(128, 4, (4, 5, 6, 7), 1)
    triples = []
    for head in range(HEADS):
        k, v = (slice(i * 256 + head * 128, i * 256 + head * 128 + 128) for i in range(2))
        for block in range(2):
            mine = slice(block * 128, block * 128 + 128)
            its = slice((block ^ 1) * 128, (block ^ 1) * 128 + 128)
            triples.append((q4[mine, k], kv4[its, k], kv4[its, v]))
        triples.append((q5[:, k], kv5[:, k], kv5[:, v]))
        triples.append((q6[:, k], kv6[:, k], kv6[:, v]))
        triples.append((q7[:, k], kv7[:, k], kv7[:, v]))
    done = attend_all(triples)
    parts = []
    for head in range(HEADS):
        k, v = (slice(i * 256 + head * 128, i * 256 + head * 128 + 128) for i in range(2))
        (oa, ea), (ob, eb), (o5, e5), (o6, e6), (o7, e7) = done[head * 5 : head * 5 + 5]
        for run in range(4):
            its = slice((run ^ 1) * 128, (run ^ 1) * 128 + 128)
            mine = slice(run * 128, run * 128 + 128)
            half = slice(run % 2 * 64, run % 2 * 64 + 64)
            values = jnp.concatenate(
                [
                    (oa, ob)[run // 2][half].astype(F32),
                    o5[run * 32 : run * 32 + 32].astype(F32),
                    o6[run * 16 : run * 16 + 16].astype(F32),
                    o7.astype(F32)[run * 8 : run * 8 + 8],
                    jnp.zeros((8, DH), F32),
                ],
                0,
            ).astype(BF)
            total = jnp.concatenate(
                [
                    (ea, eb)[run // 2][half],
                    e5[run * 32 : run * 32 + 32],
                    e6[run * 16 : run * 16 + 16],
                    e7[run * 8 : run * 8 + 8],
                    jnp.zeros((8, DH), F32),
                ],
                0,
            )
            parts.append((q3[mine, k], kv3[its, k], kv3[its, v], level_row(total), values, None))
    for index, (weighted, total, highest) in enumerate(merged(parts, found)):
        head, run = divmod(index, 4)
        c = slice(head * 128, head * 128 + 128)
        o3[run * 128 : run * 128 + 128, c] = quotient(weighted, total).astype(BF)
        ends = level_row(highest + jnp.log2(total))
        lanes = [
            jnp.concatenate(
                [jnp.zeros((1, 96), F32), ends[:, block * 16 : block * 16 + 16], jnp.zeros((1, 16), F32)], 1
            )
            for block in range(8)
        ]
        mine = slice(run * 8, run * 8 + 8)
        virtual_3[mine, c] = jnp.concatenate(lanes, 0) + virtual[mine, c]

    found = level_matches(128, 1, (1, 2, 3), 1)
    row = iota((8, 128), 0)

    @pl.loop(0, RUNS)
    def _(step):
        first = jnp.where((step == 0) & (edge[1] == 1), GONE, 0.0)
        last = jnp.where((step == 3) & (edge[2] == 1), GONE, 0.0)
        gathered = jnp.zeros((8, 128), F32)
        levels = virtual_3[pl.ds(pl.multiple_of(step * 8, 8), 8), :]
        for group in range(8 // GROUP):
            parts = []
            for block in range(group * GROUP, group * GROUP + GROUP):
                at = pl.multiple_of(step * TM + block * 128, 128)
                b = step * 8 + block
                at1 = pl.ds(pl.multiple_of(b * 64, 64), 64)
                at2 = pl.ds(pl.multiple_of(b * 32, 32), 32)
                at3 = pl.ds(pl.multiple_of(b * 16, 16), 16)
                bias = None
                if block == 0:
                    bias = jnp.where(iota((1, 384), 1) < 128, first, 0.0)
                    before = pl.multiple_of(jnp.maximum(at - 128, 0), 128)
                    window = jnp.concatenate(
                        [jnp.where(step == 0, above, kv[pl.ds(before, 128), :]), kv[pl.ds(at, 256), :]], 0
                    )
                elif block == 7:
                    after = pl.multiple_of(jnp.minimum(at + 128, TOKENS - 128), 128)
                    window = jnp.concatenate(
                        [
                            kv[pl.ds(pl.multiple_of(at - 128, 128), 256), :],
                            jnp.where(step == RUNS - 1, below, kv[pl.ds(after, 128), :]),
                        ],
                        0,
                    )
                else:
                    window = kv.at[pl.ds(pl.multiple_of(at - 128, 128), 384)]
                if block == 7:
                    bias = jnp.where(iota((1, 384), 1) >= 256, last, 0.0)
                for head in range(HEADS):
                    c, gv = (slice(i * 256 + head * 128, i * 256 + head * 128 + 128) for i in range(2))
                    values = jnp.concatenate(
                        [o1[at1, c], o2[at2, c], o3[at3, c], jnp.zeros((16, DH), BF)], 0
                    )
                    parts.append(
                        (
                            q[pl.ds(at, 128), c],
                            window[:, c],
                            window[:, gv],
                            levels[block : block + 1, c],
                            values,
                            bias,
                        )
                    )
            done = merged(parts, found)
            for index, block in enumerate(range(group * GROUP, group * GROUP + GROUP)):
                sums = jnp.zeros((128, DH), F32)
                at = pl.ds(pl.multiple_of(step * TM + block * 128, 128), 128)
                for head in range(HEADS):
                    weighted, total, _ = done[index * HEADS + head]
                    attention = quotient(weighted, total)
                    out[at, head * 128 : head * 128 + 128] = attention.astype(BF)
                    sums = sums + attention * attention
                token_sums = dot_t(jnp.ones((8, DH), F32), sums)
                gathered = jnp.where(row == block, token_sums, gathered)
        squares[pl.ds(pl.multiple_of(step * 8, 8), 8), :] = gathered


def fine(edge, *arrays):
    local = pl.BlockSpec(memory_space=pltpu.VMEM)
    shape = jax.ShapeDtypeStruct
    return pl.pallas_call(
        fine_kernel,
        in_specs=[pl.BlockSpec(memory_space=pltpu.SMEM)] + [local] * len(arrays),
        out_specs=[local, local],
        scratch_shapes=[pltpu.VMEM((512, 256), BF), pltpu.VMEM((32, 256), F32)],
        out_shape=[shape((TOKENS, 256), BF), shape((32, 128), F32)],
        compiler_params=pltpu.CompilerParams(vmem_limit_bytes=VMEM_LIMIT),
        name="merge_levels",
        cost_estimate=pl.CostEstimate(
            flops=4 * TOKENS * 512 * 256, bytes_accessed=18 * 2**20, transcendentals=TOKENS * 1024
        ),
    )(edge, *arrays)


def norm_kernel(rows, s0, s1, s2, s3, gain, out, done, out_sem):
    leaving = parts_of(done, out, out_sem, 8)
    total = s0[...] + s1[...] + s2[...] + s3[...]
    factor = lax.rsqrt(total / D + 1e-6)
    eye = iota((128, 128), 0) == iota((128, 128), 1)
    for part in range(8):
        for block in range(part * 4, part * 4 + 4):
            mine = slice(block * 128, block * 128 + 128)
            column = jnp.sum(jnp.where(eye, factor[block : block + 1], 0.0), axis=1, keepdims=True)
            done[mine, :] = (rows[mine, :].astype(F32) * column * gain[...]).astype(BF)
        leaving[part].start()
    wait_all(leaving)


def norm(attention, sums, gain):
    local = pl.BlockSpec(memory_space=pltpu.VMEM)
    return pl.pallas_call(
        norm_kernel,
        in_specs=[local] * 6,
        out_specs=pl.BlockSpec(memory_space=pl.ANY),
        out_shape=jax.ShapeDtypeStruct((TOKENS, 256), BF),
        scratch_shapes=[pltpu.VMEM((TOKENS, 256), BF), pltpu.SemaphoreType.DMA((8,))],
        compiler_params=pltpu.CompilerParams(vmem_limit_bytes=16 * 2**20),
        name="norm",
    )(attention, *sums, gain)


def join_kernel(a, b, c, out):
    out[:, :256] = a[...]
    out[:, 256:512] = b[...]
    out[:, 512:] = c[...]


def joined(*weights):
    local = pl.BlockSpec(memory_space=pltpu.VMEM)
    return pl.pallas_call(
        join_kernel,
        in_specs=[local] * 3,
        out_specs=local,
        out_shape=jax.ShapeDtypeStruct((128, 768), BF),
        name="join_weights",
    )(*weights)


def shards(hidden_states, w_query, w_key, w_value, norm_gain):
    position = lax.axis_index("seq")
    core = lax.axis_index("head") % 2
    x, z = position // SIDE, position % SIDE
    w_mine = joined(w_key, w_value, w_query)
    line = jnp.stack([w_mine] + [along_line(w_mine, True, s) for s in SHIFTS])
    line_kv, line_q = line[:, :, :512], line[:, :, 512:]
    pieces_kv = [line_kv] + [along_line(line_kv, False, s) for s in SHIFTS]
    pieces_q = [line_q] + [along_line(line_q, False, s) for s in SHIFTS]
    back = jnp.array((0,) + SHIFTS, jnp.int32)
    near_x = jnp.where(core == 0, (x - back[:, None]) % SIDE, (x - back[None, :]) % SIDE)
    near_z = jnp.where(core == 0, (z - back[None, :]) % SIDE, (z - back[:, None]) % SIDE)
    place = jnp.concatenate([(near_x * SIDE + near_z).reshape(16), (position % 2).reshape(1)])
    place = place.astype(jnp.int32)
    kv, kv1, kv2, kv3, kv4, send_a, send_b, send_6, send_7 = project_keys(place, hidden_states, pieces_kv)
    got_d = flipped(send_7, 4)
    got_a = flipped(send_a, 1)
    got_b = other_side(send_b)
    far = jnp.concatenate([send_6, got_d], 0)
    got_s = flipped(got_d, 1)
    got_c = flipped(far, 2)
    got_e = flipped(far, 3)
    q, o1, o2, virtual, q3, q4, q5, q6, q7 = project_queries(place, hidden_states, pieces_q, kv1, kv2)
    edge = jnp.stack([position % 2, position == 0, position == 15]).astype(jnp.int32)
    attention, squares = fine(
        edge, q3, kv3, q4, kv4, q5, q6, q7, got_a, got_b, got_d, got_s, got_c, got_e, virtual, q, kv, o1, o2
    )
    chip = squares + over_heads(squares, lambda i: i ^ 1)
    sums = [chip] + [over_heads(chip, lambda i, s=s: (i + 2 * s) % 8) for s in SHIFTS]
    return norm(attention, sums, norm_gain.reshape(1, 256))


def solution(mesh):
    in_specs = (P("seq", None), P("seq", "head"), P("seq", "head"), P("seq", "head"), P("head"))
    return jax.shard_map(
        shards, mesh=mesh, in_specs=in_specs, out_specs=P("seq", "head"), check_vma=False
    )
```

```python
import jax
import jax.numpy as jnp
import numpy as np
from jax import lax
from jax.experimental import pallas as pl
from jax.experimental.pallas import tpu as pltpu
from jax.sharding import PartitionSpec as P

H = 16
DH = 128
B = 128
D = 2048
HEADS = 2
SIDE = 4
TOKENS = 4096
SCALE = float(DH**-0.5 * np.log2(np.e))
GONE = -1e30
SHIFTS = (1, 3, 2)
BF = jnp.bfloat16
F32 = jnp.float32
TM = 1024
CHUNK = 512
CHUNKS = TOKENS // CHUNK
RUNS = TOKENS // TM
VMEM_LIMIT = 32 * 2**20
EARLY_LIMIT = 32 * 2**20
LATE_LIMIT = 32 * 2**20
GROUP = 8


def line_perm(first, shift):
    pairs = []
    for x in range(SIDE):
        for z in range(SIDE):
            for head in range(8):
                if (head % 2 == 0) == first:
                    target = x * SIDE + (z + shift) % SIDE
                else:
                    target = (x + shift) % SIDE * SIDE + z
                pairs.append(((x * SIDE + z) * 8 + head, target * 8 + head))
    return pairs


def along_line(value, first, shift):
    return lax.ppermute(value, ("seq", "head"), line_perm(first, shift))


def flipped(value, bits):
    return lax.ppermute(value, "seq", [(i, i ^ bits) for i in range(16)])


def other_side(value):
    pairs = [(i, i + 1) for i in range(1, 15, 2)] + [(i + 1, i) for i in range(1, 15, 2)]
    return lax.ppermute(value, "seq", pairs)


def over_heads(value, step):
    return lax.ppermute(value, "head", [(i, step(i)) for i in range(8)])


def dot(a, b):
    return lax.dot_general(a, b, (((1,), (0,)), ((), ())), preferred_element_type=F32)


def dot_t(a, b):
    return lax.dot_general(a, b, (((1,), (1,)), ((), ())), preferred_element_type=F32)


def iota(shape, dim):
    return lax.broadcasted_iota(jnp.int32, shape, dim)


def level_matches(rows, first, levels, row_dim):
    shape = (128, rows) if row_dim == 1 else (rows, rows)
    token, slot = iota(shape, 0), iota(shape, 1)
    found = jnp.zeros(shape, jnp.bool_)
    start = 0
    for level in levels:
        count = 128 >> (level - first + 1)
        found = found | ((slot - start) == (token >> (level - first + 1)))  & (slot >= start) & (
            slot < start + count
        )
        start += count
    return found


def pool_matrix(rows, tokens, levels, first=0):
    row, token = iota((rows, tokens), 0), iota((rows, tokens), 1)
    total = jnp.zeros((rows, tokens), F32)
    start = 0
    for level in levels:
        count = tokens >> (level - first)
        inside = (row >= start) & (row < start + count) & ((row - start) == (token >> (level - first)))
        total = jnp.where(inside, 2.0 ** (first - level), total)
        start += count
    return total.astype(BF)


def parts_of(source, target, sems, count):
    rows = source.shape[0] // count
    return [
        pltpu.make_async_copy(
            source.at[pl.ds(i * rows, rows)], target.at[pl.ds(i * rows, rows)], sems.at[i]
        )
        for i in range(count)
    ]


def part_of(source, target, sems, index, rows):
    at = pl.ds(pl.multiple_of(index * rows, rows), rows)
    return pltpu.make_async_copy(source.at[at], target.at[at], sems.at[index])


def start_all(copies):
    for copy in copies:
        copy.start()


def wait_all(copies):
    for copy in copies:
        copy.wait()


def half_rows(place, base, hidden, ring, h_sem, index):
    rows = pl.ds(pl.multiple_of(index * CHUNK, CHUNK), CHUNK)
    slot = index % 3
    return [
        pltpu.make_async_copy(
            hidden.at[rows, pl.ds(pl.multiple_of(place[base + block] * 128, 128), 128)],
            ring.at[slot, :, pl.ds(block * 128, 128)],
            h_sem.at[slot, block],
        )
        for block in range(ring.shape[2] // 128)
    ]


def next_half(place, base, hidden, ring, h_sem, index):
    wait_all(half_rows(place, base, hidden, ring, h_sem, index))

    @pl.when(index < CHUNKS - 2)
    def _():
        start_all(half_rows(place, base, hidden, ring, h_sem, index + 2))


def join_half(pieces, w_half):
    for n, piece in enumerate(pieces):
        for i in range(SIDE):
            w_half[(n * SIDE + i) * 128 : (n * SIDE + i + 1) * 128, :] = piece[i]


def pool_runs(l3):
    p_coarse = pool_matrix(128, 128, (4, 5, 6, 7), 3)
    coarse = [dot(p_coarse, l3[run * 128 : run * 128 + 128, :]) for run in range(4)]
    return [
        jnp.concatenate([c[low:high] for c in coarse], 0).astype(BF)
        for low, high in ((0, 64), (64, 96), (96, 112), (112, 120))
    ]


def early_kernel(place, hidden, w0, w1, w2, sums, ring, w_half, h_sem):
    for index in range(2):
        start_all(half_rows(place, 0, hidden, ring, h_sem, index))
    join_half((w0, w1, w2), w_half)

    @pl.loop(0, CHUNKS)
    def _(index):
        next_half(place, 0, hidden, ring, h_sem, index)
        at = pl.ds(pl.multiple_of(index * CHUNK, CHUNK), CHUNK)
        sums[at, :] = dot(ring[index % 3], w_half[...]).astype(BF)


def late_kernel(
    place, hidden, w3, sums,
    kv, kv1, kv2, kv3, kv4, q, q1, q2, q3, q4, q5, q6, q7, send_a, send_b, six, seven,
    ring, w_half, l3, h_sem,
):
    for index in range(2):
        start_all(half_rows(place, 12, hidden, ring, h_sem, index))
    join_half((w3,), w_half)
    p_fine = pool_matrix(112, 128, (1, 2, 3))

    def pool(index):
        at = pl.ds(pl.multiple_of(index * CHUNK, CHUNK), CHUNK)
        rows = jnp.concatenate([kv[at, :], q[at, :]], 1)
        pooled = [
            dot(p_fine, rows[part * 128 : part * 128 + 128]).astype(BF) for part in range(CHUNK // 128)
        ]
        for part, means in enumerate(pooled):
            block = index * (CHUNK // 128) + part
            at1 = pl.ds(pl.multiple_of(block * 64, 64), 64)
            at2 = pl.ds(pl.multiple_of(block * 32, 32), 32)
            at3 = pl.ds(pl.multiple_of(block * 16, 16), 16)
            kv1[at1, :] = means[:64, :512]
            q1[at1, :] = means[:64, 512:]
            kv2[at2, :] = means[64:96, :512]
            q2[at2, :] = means[64:96, 512:]
            l3[at3, :] = means[96:112]

    def project(index):
        next_half(place, 12, hidden, ring, h_sem, index)
        at = pl.ds(pl.multiple_of(index * CHUNK, CHUNK), CHUNK)
        rows = (dot(ring[index % 3], w_half[...]) + sums[at, :].astype(F32)).astype(BF)
        return at, rows

    at, rows = project(jnp.int32(0))
    kv[at, :] = rows[:, :512]
    q[at, :] = rows[:, 512:]

    @pl.loop(1, CHUNKS)
    def _(index):
        at, rows = project(index)
        pool(index - 1)
        kv[at, :] = rows[:, :512]
        q[at, :] = rows[:, 512:]

    pool(CHUNKS - 1)
    kv3[...] = l3[:, :512]
    q3[...] = l3[:, 512:]
    four, five, last, tail = pool_runs(l3)
    kv4[...] = four[:, :512]
    q4[...] = four[:, 512:]
    q5[...] = five[:, 512:]
    q6[...] = last[:, 512:]
    q7[...] = tail[:, 512:]
    six[...] = last[:, :512]
    seven[...] = tail[:, :512]
    odd = place[16] == 1
    low, high = kv[:128, :], kv[TOKENS - 128 :, :]
    send_a[:128, :] = jnp.where(odd, low, high)
    send_b[...] = jnp.where(odd, high, low)
    send_a[128:, :] = five[:, :512]


def project_early(place, hidden, pieces):
    anywhere = pl.BlockSpec(memory_space=pl.ANY)
    local = pl.BlockSpec(memory_space=pltpu.VMEM)
    return pl.pallas_call(
        early_kernel,
        in_specs=[pl.BlockSpec(memory_space=pltpu.SMEM), anywhere] + [local] * 3,
        out_specs=local,
        out_shape=jax.ShapeDtypeStruct((TOKENS, 768), BF),
        scratch_shapes=[
            pltpu.VMEM((3, CHUNK, 1536), BF),
            pltpu.VMEM((1536, 768), BF),
            pltpu.SemaphoreType.DMA((3, 12)),
        ],
        compiler_params=pltpu.CompilerParams(vmem_limit_bytes=EARLY_LIMIT),
        name="project_early",
        cost_estimate=pl.CostEstimate(
            flops=3 * TOKENS * 1024 * 768, bytes_accessed=12 * 2**20, transcendentals=0
        ),
    )(place, hidden, *pieces)


def project_late(place, hidden, pieces, sums):
    anywhere = pl.BlockSpec(memory_space=pl.ANY)
    local = pl.BlockSpec(memory_space=pltpu.VMEM)
    sizes = [(TOKENS >> level, 512) for level in range(5)]
    sizes += [(TOKENS >> level, 256) for level in range(8)]
    sizes += [(256, 512), (128, 512), (64, 512), (32, 512)]
    return pl.pallas_call(
        late_kernel,
        in_specs=[pl.BlockSpec(memory_space=pltpu.SMEM), anywhere] + [local] * 2,
        out_specs=[local] * len(sizes),
        out_shape=[jax.ShapeDtypeStruct(size, BF) for size in sizes],
        scratch_shapes=[
            pltpu.VMEM((3, CHUNK, 512), BF),
            pltpu.VMEM((512, 768), BF),
            pltpu.VMEM((512, 768), BF),
            pltpu.SemaphoreType.DMA((3, 4)),
        ],
        compiler_params=pltpu.CompilerParams(vmem_limit_bytes=LATE_LIMIT),
        name="project_late",
        cost_estimate=pl.CostEstimate(
            flops=TOKENS * 1024 * 768, bytes_accessed=8 * 2**20, transcendentals=0
        ),
    )(place, hidden, *pieces, sums)


def pairs_kernel(q1, kv1, q2, kv2, o1, o2, virtual):
    for run in range(RUNS):
        triples, places = [], []
        for head in range(HEADS):
            k, v = (slice(i * 256 + head * 128, i * 256 + head * 128 + 128) for i in range(2))
            for q_all, kv_all, out, count in ((q1, kv1, o1, 4), (q2, kv2, o2, 2)):
                for block in range(run * count, run * count + count):
                    mine = slice(block * 128, block * 128 + 128)
                    its = slice((block ^ 1) * 128, (block ^ 1) * 128 + 128)
                    triples.append((q_all[mine, k], kv_all[its, k], kv_all[its, v]))
                    places.append((out, mine, k))
        done = attend_all(triples)
        for (out, mine, k), (rows, _) in zip(places, done):
            out[mine, k] = rows
        for head in range(HEADS):
            ends = [level_row(total) for _, total in done[head * 6 : head * 6 + 6]]
            lanes = []
            for block in range(8):
                fine = ends[block // 2][:, block % 2 * 64 : block % 2 * 64 + 64]
                coarse = ends[4 + block // 4][:, block % 4 * 32 : block % 4 * 32 + 32]
                lanes.append(jnp.concatenate([fine, coarse, jnp.zeros((1, 32), F32)], 1))
            virtual[run * 8 : run * 8 + 8, head * 128 : head * 128 + 128] = jnp.concatenate(lanes, 0)


def pairs(*arrays):
    local = pl.BlockSpec(memory_space=pltpu.VMEM)
    shape = jax.ShapeDtypeStruct
    return pl.pallas_call(
        pairs_kernel,
        in_specs=[local] * 4,
        out_specs=[local] * 3,
        out_shape=[shape((2048, 256), BF), shape((1024, 256), BF), shape((32, 256), F32)],
        compiler_params=pltpu.CompilerParams(vmem_limit_bytes=VMEM_LIMIT),
        name="levels_1_2",
        cost_estimate=pl.CostEstimate(
            flops=2 * 3072 * 128 * 512, bytes_accessed=9 * 2**20, transcendentals=3072 * 256
        ),
    )(*arrays)


def with_ones(values):
    return jnp.concatenate([values, jnp.ones_like(values)], axis=1)


def quotient(rows, total):
    inverse = pl.reciprocal(total, approx=True)
    return rows * (inverse * (2.0 - total * inverse))


def attend_all(triples):
    scores = [dot_t(queries, key_rows) * SCALE for queries, key_rows, _ in triples]
    highest = [jnp.max(s, axis=1, keepdims=True) for s in scores]
    weights = [jnp.exp2(s - h).astype(BF) for s, h in zip(scores, highest)]
    both = [dot(w, with_ones(values)) for w, (_, _, values) in zip(weights, triples)]
    return [
        (quotient(o[:, :DH], o[:, DH:]).astype(BF), h + jnp.log2(o[:, DH:])) for o, h in zip(both, highest)
    ]


def level_row(total):
    eye = iota((128, 128), 0) == iota((128, 128), 1)
    return jnp.sum(jnp.where(eye, total, 0.0), axis=0, keepdims=True)


def merged(parts, found):
    scores = [dot_t(queries, key_rows) * SCALE for queries, key_rows, *_ in parts]
    scores = [s if p[5] is None else s + p[5] for s, p in zip(scores, parts)]
    coarse = [jnp.where(found, p[3], GONE) for p in parts]
    highest = [
        jnp.maximum(jnp.max(s, axis=1, keepdims=True), jnp.max(c, axis=1, keepdims=True))
        for s, c in zip(scores, coarse)
    ]
    weights = [
        jnp.concatenate([jnp.exp2(s - h).astype(BF), jnp.exp2(c - h).astype(BF)], 1)
        for s, c, h in zip(scores, coarse, highest)
    ]
    both = [
        dot(w, with_ones(jnp.concatenate([p[2], p[4]], 0))) for w, p in zip(weights, parts)
    ]
    return [(o[:, :DH], o[:, DH:], h) for o, h in zip(both, highest)]


def fine_kernel(
    edge, q3, kv3, q4, kv4, q5, q6, q7, got_a, got_b, got_d, got_s, got_c, got_e, virtual, q, kv, o1, o2,
    out, squares, o3, virtual_3,
):
    odd = edge[0] == 1
    kv5 = got_a.at[pl.ds(128, 128)]
    kv6 = jnp.concatenate([got_c[:64, :], got_e[:64, :]], 0)
    kv7 = jnp.concatenate([got_d[...], got_s[...], got_c[64:, :], got_e[64:, :]], 0)
    above = jnp.where(odd, got_a[:128, :], got_b[...])
    below = jnp.where(odd, got_b[...], got_a[:128, :])
    found = level_matches(128, 4, (4, 5, 6, 7), 1)
    triples = []
    for head in range(HEADS):
        k, v = (slice(i * 256 + head * 128, i * 256 + head * 128 + 128) for i in range(2))
        for block in range(2):
            mine = slice(block * 128, block * 128 + 128)
            its = slice((block ^ 1) * 128, (block ^ 1) * 128 + 128)
            triples.append((q4[mine, k], kv4[its, k], kv4[its, v]))
        triples.append((q5[:, k], kv5[:, k], kv5[:, v]))
        triples.append((q6[:, k], kv6[:, k], kv6[:, v]))
        triples.append((q7[:, k], kv7[:, k], kv7[:, v]))
    done = attend_all(triples)
    parts = []
    for head in range(HEADS):
        k, v = (slice(i * 256 + head * 128, i * 256 + head * 128 + 128) for i in range(2))
        (oa, ea), (ob, eb), (o5, e5), (o6, e6), (o7, e7) = done[head * 5 : head * 5 + 5]
        for run in range(4):
            its = slice((run ^ 1) * 128, (run ^ 1) * 128 + 128)
            mine = slice(run * 128, run * 128 + 128)
            half = slice(run % 2 * 64, run % 2 * 64 + 64)
            values = jnp.concatenate(
                [
                    (oa, ob)[run // 2][half].astype(F32),
                    o5[run * 32 : run * 32 + 32].astype(F32),
                    o6[run * 16 : run * 16 + 16].astype(F32),
                    o7.astype(F32)[run * 8 : run * 8 + 8],
                    jnp.zeros((8, DH), F32),
                ],
                0,
            ).astype(BF)
            total = jnp.concatenate(
                [
                    (ea, eb)[run // 2][half],
                    e5[run * 32 : run * 32 + 32],
                    e6[run * 16 : run * 16 + 16],
                    e7[run * 8 : run * 8 + 8],
                    jnp.zeros((8, DH), F32),
                ],
                0,
            )
            parts.append((q3[mine, k], kv3[its, k], kv3[its, v], level_row(total), values, None))
    for index, (weighted, total, highest) in enumerate(merged(parts, found)):
        head, run = divmod(index, 4)
        c = slice(head * 128, head * 128 + 128)
        o3[run * 128 : run * 128 + 128, c] = quotient(weighted, total).astype(BF)
        ends = level_row(highest + jnp.log2(total))
        lanes = [
            jnp.concatenate(
                [jnp.zeros((1, 96), F32), ends[:, block * 16 : block * 16 + 16], jnp.zeros((1, 16), F32)], 1
            )
            for block in range(8)
        ]
        mine = slice(run * 8, run * 8 + 8)
        virtual_3[mine, c] = jnp.concatenate(lanes, 0) + virtual[mine, c]

    found = level_matches(128, 1, (1, 2, 3), 1)
    row = iota((8, 128), 0)

    @pl.loop(0, RUNS)
    def _(step):
        first = jnp.where((step == 0) & (edge[1] == 1), GONE, 0.0)
        last = jnp.where((step == 3) & (edge[2] == 1), GONE, 0.0)
        gathered = jnp.zeros((8, 128), F32)
        levels = virtual_3[pl.ds(pl.multiple_of(step * 8, 8), 8), :]
        for group in range(8 // GROUP):
            parts = []
            for block in range(group * GROUP, group * GROUP + GROUP):
                at = pl.multiple_of(step * TM + block * 128, 128)
                b = step * 8 + block
                at1 = pl.ds(pl.multiple_of(b * 64, 64), 64)
                at2 = pl.ds(pl.multiple_of(b * 32, 32), 32)
                at3 = pl.ds(pl.multiple_of(b * 16, 16), 16)
                bias = None
                if block == 0:
                    bias = jnp.where(iota((1, 384), 1) < 128, first, 0.0)
                    before = pl.multiple_of(jnp.maximum(at - 128, 0), 128)
                    window = jnp.concatenate(
                        [jnp.where(step == 0, above, kv[pl.ds(before, 128), :]), kv[pl.ds(at, 256), :]], 0
                    )
                elif block == 7:
                    after = pl.multiple_of(jnp.minimum(at + 128, TOKENS - 128), 128)
                    window = jnp.concatenate(
                        [
                            kv[pl.ds(pl.multiple_of(at - 128, 128), 256), :],
                            jnp.where(step == RUNS - 1, below, kv[pl.ds(after, 128), :]),
                        ],
                        0,
                    )
                else:
                    window = kv.at[pl.ds(pl.multiple_of(at - 128, 128), 384)]
                if block == 7:
                    bias = jnp.where(iota((1, 384), 1) >= 256, last, 0.0)
                for head in range(HEADS):
                    c, gv = (slice(i * 256 + head * 128, i * 256 + head * 128 + 128) for i in range(2))
                    values = jnp.concatenate(
                        [o1[at1, c], o2[at2, c], o3[at3, c], jnp.zeros((16, DH), BF)], 0
                    )
                    parts.append(
                        (
                            q[pl.ds(at, 128), c],
                            window[:, c],
                            window[:, gv],
                            levels[block : block + 1, c],
                            values,
                            bias,
                        )
                    )
            done = merged(parts, found)
            for index, block in enumerate(range(group * GROUP, group * GROUP + GROUP)):
                sums = jnp.zeros((128, DH), F32)
                at = pl.ds(pl.multiple_of(step * TM + block * 128, 128), 128)
                for head in range(HEADS):
                    weighted, total, _ = done[index * HEADS + head]
                    attention = quotient(weighted, total)
                    out[at, head * 128 : head * 128 + 128] = attention.astype(BF)
                    sums = sums + attention * attention
                token_sums = dot_t(jnp.ones((8, DH), F32), sums)
                gathered = jnp.where(row == block, token_sums, gathered)
        squares[pl.ds(pl.multiple_of(step * 8, 8), 8), :] = gathered


def fine(edge, *arrays):
    local = pl.BlockSpec(memory_space=pltpu.VMEM)
    shape = jax.ShapeDtypeStruct
    return pl.pallas_call(
        fine_kernel,
        in_specs=[pl.BlockSpec(memory_space=pltpu.SMEM)] + [local] * len(arrays),
        out_specs=[local, local],
        scratch_shapes=[pltpu.VMEM((512, 256), BF), pltpu.VMEM((32, 256), F32)],
        out_shape=[shape((TOKENS, 256), BF), shape((32, 128), F32)],
        compiler_params=pltpu.CompilerParams(vmem_limit_bytes=VMEM_LIMIT),
        name="merge_levels",
        cost_estimate=pl.CostEstimate(
            flops=4 * TOKENS * 512 * 256, bytes_accessed=18 * 2**20, transcendentals=TOKENS * 1024
        ),
    )(edge, *arrays)


def norm_kernel(rows, s0, s1, s2, s3, gain, out, done, out_sem):
    leaving = parts_of(done, out, out_sem, 8)
    total = s0[...] + s1[...] + s2[...] + s3[...]
    factor = lax.rsqrt(total / D + 1e-6)
    eye = iota((128, 128), 0) == iota((128, 128), 1)
    for part in range(8):
        for block in range(part * 4, part * 4 + 4):
            mine = slice(block * 128, block * 128 + 128)
            column = jnp.sum(jnp.where(eye, factor[block : block + 1], 0.0), axis=1, keepdims=True)
            done[mine, :] = (rows[mine, :].astype(F32) * column * gain[...]).astype(BF)
        leaving[part].start()
    wait_all(leaving)


def norm(attention, sums, gain):
    local = pl.BlockSpec(memory_space=pltpu.VMEM)
    return pl.pallas_call(
        norm_kernel,
        in_specs=[local] * 6,
        out_specs=pl.BlockSpec(memory_space=pl.ANY),
        out_shape=jax.ShapeDtypeStruct((TOKENS, 256), BF),
        scratch_shapes=[pltpu.VMEM((TOKENS, 256), BF), pltpu.SemaphoreType.DMA((8,))],
        compiler_params=pltpu.CompilerParams(vmem_limit_bytes=16 * 2**20),
        name="norm",
    )(attention, *sums, gain)


def join_kernel(a, b, c, out):
    out[:, :256] = a[...]
    out[:, 256:512] = b[...]
    out[:, 512:] = c[...]


def joined(*weights):
    local = pl.BlockSpec(memory_space=pltpu.VMEM)
    return pl.pallas_call(
        join_kernel,
        in_specs=[local] * 3,
        out_specs=local,
        out_shape=jax.ShapeDtypeStruct((128, 768), BF),
        name="join_weights",
    )(*weights)


def shards(hidden_states, w_query, w_key, w_value, norm_gain):
    position = lax.axis_index("seq")
    core = lax.axis_index("head") % 2
    x, z = position // SIDE, position % SIDE
    w_mine = joined(w_key, w_value, w_query)
    line = jnp.stack([w_mine] + [along_line(w_mine, True, s) for s in SHIFTS])
    pieces = [line] + [along_line(line, False, s) for s in SHIFTS[:2]]
    *pieces, line = lax.optimization_barrier((*pieces, line))
    pieces = [*pieces, along_line(line, False, SHIFTS[2])]
    back = jnp.array((0,) + SHIFTS, jnp.int32)
    near_x = jnp.where(core == 0, (x - back[:, None]) % SIDE, (x - back[None, :]) % SIDE)
    near_z = jnp.where(core == 0, (z - back[None, :]) % SIDE, (z - back[:, None]) % SIDE)
    place = jnp.concatenate([(near_x * SIDE + near_z).reshape(16), (position % 2).reshape(1)])
    place = place.astype(jnp.int32)
    sums = project_early(place, hidden_states, pieces[:3])
    kv, kv1, kv2, kv3, kv4, q, q1, q2, q3, q4, q5, q6, q7, send_a, send_b, send_6, send_7 = project_late(
        place, hidden_states, pieces[3:], sums
    )
    got_d = flipped(send_7, 4)
    got_a = flipped(send_a, 1)
    got_b = other_side(send_b)
    far = jnp.concatenate([send_6, got_d], 0)
    got_s = flipped(got_d, 1)
    got_c = flipped(far, 2)
    got_e = flipped(far, 3)
    o1, o2, virtual = pairs(q1, kv1, q2, kv2)
    edge = jnp.stack([position % 2, position == 0, position == 15]).astype(jnp.int32)
    attention, squares = fine(
        edge, q3, kv3, q4, kv4, q5, q6, q7, got_a, got_b, got_d, got_s, got_c, got_e, virtual, q, kv, o1, o2
    )
    chip = squares + over_heads(squares, lambda i: i ^ 1)
    sums = [chip] + [over_heads(chip, lambda i, s=s: (i + 2 * s) % 8) for s in SHIFTS]
    return norm(attention, sums, norm_gain.reshape(1, 256))


def solution(mesh):
    in_specs = (P("seq", None), P("seq", "head"), P("seq", "head"), P("seq", "head"), P("head"))
    return jax.shard_map(
        shards, mesh=mesh, in_specs=in_specs, out_specs=P("seq", "head"), check_vma=False
    )
```

```python
import jax
import jax.numpy as jnp
import numpy as np
from jax import lax
from jax.experimental import pallas as pl
from jax.experimental.pallas import tpu as pltpu
from jax.sharding import PartitionSpec as P

H = 16
DH = 128
B = 128
D = 2048
HEADS = 2
SIDE = 4
TOKENS = 4096
SCALE = float(DH**-0.5 * np.log2(np.e))
GONE = -1e30
SHIFTS = (1, 3, 2)
BF = jnp.bfloat16
F32 = jnp.float32
TM = 1024
CHUNK = 1024
CHUNKS = TOKENS // CHUNK
RUNS = TOKENS // TM
VMEM_LIMIT = 32 * 2**20
EARLY_LIMIT = 28 * 2**20
LATE_LIMIT = 20 * 2**20
GROUP = 8


def line_perm(first, shift):
    pairs = []
    for x in range(SIDE):
        for z in range(SIDE):
            for head in range(8):
                if (head % 2 == 0) == first:
                    target = x * SIDE + (z + shift) % SIDE
                else:
                    target = (x + shift) % SIDE * SIDE + z
                pairs.append(((x * SIDE + z) * 8 + head, target * 8 + head))
    return pairs


def along_line(value, first, shift):
    return lax.ppermute(value, ("seq", "head"), line_perm(first, shift))


def flipped(value, bits):
    return lax.ppermute(value, "seq", [(i, i ^ bits) for i in range(16)])


def other_side(value):
    pairs = [(i, i + 1) for i in range(1, 15, 2)] + [(i + 1, i) for i in range(1, 15, 2)]
    return lax.ppermute(value, "seq", pairs)


def over_heads(value, step):
    return lax.ppermute(value, "head", [(i, step(i)) for i in range(8)])


def dot(a, b):
    return lax.dot_general(a, b, (((1,), (0,)), ((), ())), preferred_element_type=F32)


def dot_t(a, b):
    return lax.dot_general(a, b, (((1,), (1,)), ((), ())), preferred_element_type=F32)


def iota(shape, dim):
    return lax.broadcasted_iota(jnp.int32, shape, dim)


def level_matches(rows, first, levels, row_dim):
    shape = (128, rows) if row_dim == 1 else (rows, rows)
    token, slot = iota(shape, 0), iota(shape, 1)
    found = jnp.zeros(shape, jnp.bool_)
    start = 0
    for level in levels:
        count = 128 >> (level - first + 1)
        found = found | ((slot - start) == (token >> (level - first + 1)))  & (slot >= start) & (
            slot < start + count
        )
        start += count
    return found


def pool_matrix(rows, tokens, levels, first=0):
    row, token = iota((rows, tokens), 0), iota((rows, tokens), 1)
    total = jnp.zeros((rows, tokens), F32)
    start = 0
    for level in levels:
        count = tokens >> (level - first)
        inside = (row >= start) & (row < start + count) & ((row - start) == (token >> (level - first)))
        total = jnp.where(inside, 2.0 ** (first - level), total)
        start += count
    return total.astype(BF)


def parts_of(source, target, sems, count):
    rows = source.shape[0] // count
    return [
        pltpu.make_async_copy(
            source.at[pl.ds(i * rows, rows)], target.at[pl.ds(i * rows, rows)], sems.at[i]
        )
        for i in range(count)
    ]


def part_of(source, target, sems, index, rows):
    at = pl.ds(pl.multiple_of(index * rows, rows), rows)
    return pltpu.make_async_copy(source.at[at], target.at[at], sems.at[index])


def start_all(copies):
    for copy in copies:
        copy.start()


def wait_all(copies):
    for copy in copies:
        copy.wait()


def half_rows(place, base, hidden, ring, h_sem, index):
    rows = pl.ds(pl.multiple_of(index * CHUNK, CHUNK), CHUNK)
    slot = index % 3
    return [
        pltpu.make_async_copy(
            hidden.at[rows, pl.ds(pl.multiple_of(place[base + block] * 128, 128), 128)],
            ring.at[slot, :, pl.ds(block * 128, 128)],
            h_sem.at[slot, block],
        )
        for block in range(ring.shape[2] // 128)
    ]


def next_half(place, base, hidden, ring, h_sem, index):
    wait_all(half_rows(place, base, hidden, ring, h_sem, index))

    @pl.when(index < CHUNKS - 2)
    def _():
        start_all(half_rows(place, base, hidden, ring, h_sem, index + 2))


def join_half(pieces, w_half):
    for n, piece in enumerate(pieces):
        for i in range(SIDE):
            w_half[(n * SIDE + i) * 128 : (n * SIDE + i + 1) * 128, :] = piece[i]


def pool_runs(l3):
    p_coarse = pool_matrix(128, 128, (4, 5, 6, 7), 3)
    coarse = [dot(p_coarse, l3[run * 128 : run * 128 + 128, :]) for run in range(4)]
    return [
        jnp.concatenate([c[low:high] for c in coarse], 0).astype(BF)
        for low, high in ((0, 64), (64, 96), (96, 112), (112, 120))
    ]


def early_kernel(place, hidden, w0, w1, w2, sums, rest, ring, w_half, h_sem, rest_sem):
    for index in range(2):
        start_all(half_rows(place, 0, hidden, ring, h_sem, index))
    join_half((w0, w1, w2), w_half)
    columns = [
        pltpu.make_async_copy(
            hidden.at[:, pl.ds(pl.multiple_of(place[12 + block] * 128, 128), 128)],
            rest.at[:, pl.ds(block * 128, 128)],
            rest_sem.at[block],
        )
        for block in range(SIDE)
    ]

    @pl.loop(0, CHUNKS)
    def _(index):
        next_half(place, 0, hidden, ring, h_sem, index)

        @pl.when(index == CHUNKS - 2)
        def _():
            start_all(columns)

        at = pl.ds(pl.multiple_of(index * CHUNK, CHUNK), CHUNK)
        sums[at, :] = dot(ring[index % 3], w_half[...]).astype(BF)

    wait_all(columns)


def late_kernel(
    place, rest, w3, sums,
    kv, kv1, kv2, kv3, kv4, q, q1, q2, q3, q4, q5, q6, q7, send_a, send_b, six, seven,
    w_half, l3,
):
    join_half((w3,), w_half)
    p_fine = pool_matrix(112, 128, (1, 2, 3))

    def pool(index):
        at = pl.ds(pl.multiple_of(index * CHUNK, CHUNK), CHUNK)
        rows = jnp.concatenate([kv[at, :], q[at, :]], 1)
        pooled = [
            dot(p_fine, rows[part * 128 : part * 128 + 128]).astype(BF) for part in range(CHUNK // 128)
        ]
        for part, means in enumerate(pooled):
            block = index * (CHUNK // 128) + part
            at1 = pl.ds(pl.multiple_of(block * 64, 64), 64)
            at2 = pl.ds(pl.multiple_of(block * 32, 32), 32)
            at3 = pl.ds(pl.multiple_of(block * 16, 16), 16)
            kv1[at1, :] = means[:64, :512]
            q1[at1, :] = means[:64, 512:]
            kv2[at2, :] = means[64:96, :512]
            q2[at2, :] = means[64:96, 512:]
            l3[at3, :] = means[96:112]

    def project(index):
        at = pl.ds(pl.multiple_of(index * CHUNK, CHUNK), CHUNK)
        rows = (dot(rest[at, :], w_half[...]) + sums[at, :].astype(F32)).astype(BF)
        return at, rows

    at, rows = project(jnp.int32(0))
    kv[at, :] = rows[:, :512]
    q[at, :] = rows[:, 512:]

    @pl.loop(1, CHUNKS)
    def _(index):
        at, rows = project(index)
        pool(index - 1)
        kv[at, :] = rows[:, :512]
        q[at, :] = rows[:, 512:]

    pool(CHUNKS - 1)
    kv3[...] = l3[:, :512]
    q3[...] = l3[:, 512:]
    four, five, last, tail = pool_runs(l3)
    kv4[...] = four[:, :512]
    q4[...] = four[:, 512:]
    q5[...] = five[:, 512:]
    q6[...] = last[:, 512:]
    q7[...] = tail[:, 512:]
    six[...] = last[:, :512]
    seven[...] = tail[:, :512]
    odd = place[16] == 1
    low, high = kv[:128, :], kv[TOKENS - 128 :, :]
    send_a[:128, :] = jnp.where(odd, low, high)
    send_b[...] = jnp.where(odd, high, low)
    send_a[128:, :] = five[:, :512]


def project_early(place, hidden, pieces):
    anywhere = pl.BlockSpec(memory_space=pl.ANY)
    local = pl.BlockSpec(memory_space=pltpu.VMEM)
    return pl.pallas_call(
        early_kernel,
        in_specs=[pl.BlockSpec(memory_space=pltpu.SMEM), anywhere] + [local] * 3,
        out_specs=[local, local],
        out_shape=[jax.ShapeDtypeStruct((TOKENS, 768), BF), jax.ShapeDtypeStruct((TOKENS, 512), BF)],
        scratch_shapes=[
            pltpu.VMEM((3, CHUNK, 1536), BF),
            pltpu.VMEM((1536, 768), BF),
            pltpu.SemaphoreType.DMA((3, 12)),
            pltpu.SemaphoreType.DMA((SIDE,)),
        ],
        compiler_params=pltpu.CompilerParams(vmem_limit_bytes=EARLY_LIMIT),
        name="project_early",
        cost_estimate=pl.CostEstimate(
            flops=3 * TOKENS * 1024 * 768, bytes_accessed=12 * 2**20, transcendentals=0
        ),
    )(place, hidden, *pieces)


def project_late(place, rest, pieces, sums):
    local = pl.BlockSpec(memory_space=pltpu.VMEM)
    sizes = [(TOKENS >> level, 512) for level in range(5)]
    sizes += [(TOKENS >> level, 256) for level in range(8)]
    sizes += [(256, 512), (128, 512), (64, 512), (32, 512)]
    return pl.pallas_call(
        late_kernel,
        in_specs=[pl.BlockSpec(memory_space=pltpu.SMEM)] + [local] * 3,
        out_specs=[local] * len(sizes),
        out_shape=[jax.ShapeDtypeStruct(size, BF) for size in sizes],
        scratch_shapes=[
            pltpu.VMEM((512, 768), BF),
            pltpu.VMEM((512, 768), BF),
        ],
        compiler_params=pltpu.CompilerParams(vmem_limit_bytes=LATE_LIMIT),
        name="project_late",
        cost_estimate=pl.CostEstimate(
            flops=TOKENS * 1024 * 768, bytes_accessed=8 * 2**20, transcendentals=0
        ),
    )(place, rest, *pieces, sums)


def pairs_kernel(q1, kv1, q2, kv2, o1, o2, virtual):
    for run in range(RUNS):
        triples, places = [], []
        for head in range(HEADS):
            k, v = (slice(i * 256 + head * 128, i * 256 + head * 128 + 128) for i in range(2))
            for q_all, kv_all, out, count in ((q1, kv1, o1, 4), (q2, kv2, o2, 2)):
                for block in range(run * count, run * count + count):
                    mine = slice(block * 128, block * 128 + 128)
                    its = slice((block ^ 1) * 128, (block ^ 1) * 128 + 128)
                    triples.append((q_all[mine, k], kv_all[its, k], kv_all[its, v]))
                    places.append((out, mine, k))
        done = attend_all(triples)
        for (out, mine, k), (rows, _) in zip(places, done):
            out[mine, k] = rows
        for head in range(HEADS):
            ends = [level_row(total) for _, total in done[head * 6 : head * 6 + 6]]
            lanes = []
            for block in range(8):
                fine = ends[block // 2][:, block % 2 * 64 : block % 2 * 64 + 64]
                coarse = ends[4 + block // 4][:, block % 4 * 32 : block % 4 * 32 + 32]
                lanes.append(jnp.concatenate([fine, coarse, jnp.zeros((1, 32), F32)], 1))
            virtual[run * 8 : run * 8 + 8, head * 128 : head * 128 + 128] = jnp.concatenate(lanes, 0)


def pairs(*arrays):
    local = pl.BlockSpec(memory_space=pltpu.VMEM)
    shape = jax.ShapeDtypeStruct
    return pl.pallas_call(
        pairs_kernel,
        in_specs=[local] * 4,
        out_specs=[local] * 3,
        out_shape=[shape((2048, 256), BF), shape((1024, 256), BF), shape((32, 256), F32)],
        compiler_params=pltpu.CompilerParams(vmem_limit_bytes=VMEM_LIMIT),
        name="levels_1_2",
        cost_estimate=pl.CostEstimate(
            flops=2 * 3072 * 128 * 512, bytes_accessed=9 * 2**20, transcendentals=3072 * 256
        ),
    )(*arrays)


def with_ones(values):
    return jnp.concatenate([values, jnp.ones_like(values)], axis=1)


def quotient(rows, total):
    inverse = pl.reciprocal(total, approx=True)
    return rows * (inverse * (2.0 - total * inverse))


def attend_all(triples):
    scores = [dot_t(queries, key_rows) * SCALE for queries, key_rows, _ in triples]
    highest = [jnp.max(s, axis=1, keepdims=True) for s in scores]
    weights = [jnp.exp2(s - h).astype(BF) for s, h in zip(scores, highest)]
    both = [dot(w, with_ones(values)) for w, (_, _, values) in zip(weights, triples)]
    return [
        (quotient(o[:, :DH], o[:, DH:]).astype(BF), h + jnp.log2(o[:, DH:])) for o, h in zip(both, highest)
    ]


def level_row(total):
    eye = iota((128, 128), 0) == iota((128, 128), 1)
    return jnp.sum(jnp.where(eye, total, 0.0), axis=0, keepdims=True)


def merged(parts, found):
    scores = [dot_t(queries, key_rows) * SCALE for queries, key_rows, *_ in parts]
    scores = [s if p[5] is None else s + p[5] for s, p in zip(scores, parts)]
    coarse = [jnp.where(found, p[3], GONE) for p in parts]
    highest = [
        jnp.maximum(jnp.max(s, axis=1, keepdims=True), jnp.max(c, axis=1, keepdims=True))
        for s, c in zip(scores, coarse)
    ]
    weights = [
        jnp.concatenate([jnp.exp2(s - h).astype(BF), jnp.exp2(c - h).astype(BF)], 1)
        for s, c, h in zip(scores, coarse, highest)
    ]
    both = [
        dot(w, with_ones(jnp.concatenate([p[2], p[4]], 0))) for w, p in zip(weights, parts)
    ]
    return [(o[:, :DH], o[:, DH:], h) for o, h in zip(both, highest)]


def fine_kernel(
    edge, q3, kv3, q4, kv4, q5, q6, q7, got_a, got_b, got_d, got_s, got_c, got_e, virtual, q, kv, o1, o2,
    out, squares, o3, virtual_3,
):
    odd = edge[0] == 1
    kv5 = got_a.at[pl.ds(128, 128)]
    kv6 = jnp.concatenate([got_c[:64, :], got_e[:64, :]], 0)
    kv7 = jnp.concatenate([got_d[...], got_s[...], got_c[64:, :], got_e[64:, :]], 0)
    above = jnp.where(odd, got_a[:128, :], got_b[...])
    below = jnp.where(odd, got_b[...], got_a[:128, :])
    found = level_matches(128, 4, (4, 5, 6, 7), 1)
    triples = []
    for head in range(HEADS):
        k, v = (slice(i * 256 + head * 128, i * 256 + head * 128 + 128) for i in range(2))
        for block in range(2):
            mine = slice(block * 128, block * 128 + 128)
            its = slice((block ^ 1) * 128, (block ^ 1) * 128 + 128)
            triples.append((q4[mine, k], kv4[its, k], kv4[its, v]))
        triples.append((q5[:, k], kv5[:, k], kv5[:, v]))
        triples.append((q6[:, k], kv6[:, k], kv6[:, v]))
        triples.append((q7[:, k], kv7[:, k], kv7[:, v]))
    done = attend_all(triples)
    parts = []
    for head in range(HEADS):
        k, v = (slice(i * 256 + head * 128, i * 256 + head * 128 + 128) for i in range(2))
        (oa, ea), (ob, eb), (o5, e5), (o6, e6), (o7, e7) = done[head * 5 : head * 5 + 5]
        for run in range(4):
            its = slice((run ^ 1) * 128, (run ^ 1) * 128 + 128)
            mine = slice(run * 128, run * 128 + 128)
            half = slice(run % 2 * 64, run % 2 * 64 + 64)
            values = jnp.concatenate(
                [
                    (oa, ob)[run // 2][half].astype(F32),
                    o5[run * 32 : run * 32 + 32].astype(F32),
                    o6[run * 16 : run * 16 + 16].astype(F32),
                    o7.astype(F32)[run * 8 : run * 8 + 8],
                    jnp.zeros((8, DH), F32),
                ],
                0,
            ).astype(BF)
            total = jnp.concatenate(
                [
                    (ea, eb)[run // 2][half],
                    e5[run * 32 : run * 32 + 32],
                    e6[run * 16 : run * 16 + 16],
                    e7[run * 8 : run * 8 + 8],
                    jnp.zeros((8, DH), F32),
                ],
                0,
            )
            parts.append((q3[mine, k], kv3[its, k], kv3[its, v], level_row(total), values, None))
    for index, (weighted, total, highest) in enumerate(merged(parts, found)):
        head, run = divmod(index, 4)
        c = slice(head * 128, head * 128 + 128)
        o3[run * 128 : run * 128 + 128, c] = quotient(weighted, total).astype(BF)
        ends = level_row(highest + jnp.log2(total))
        lanes = [
            jnp.concatenate(
                [jnp.zeros((1, 96), F32), ends[:, block * 16 : block * 16 + 16], jnp.zeros((1, 16), F32)], 1
            )
            for block in range(8)
        ]
        mine = slice(run * 8, run * 8 + 8)
        virtual_3[mine, c] = jnp.concatenate(lanes, 0) + virtual[mine, c]

    found = level_matches(128, 1, (1, 2, 3), 1)
    row = iota((8, 128), 0)

    @pl.loop(0, RUNS)
    def _(step):
        first = jnp.where((step == 0) & (edge[1] == 1), GONE, 0.0)
        last = jnp.where((step == 3) & (edge[2] == 1), GONE, 0.0)
        gathered = jnp.zeros((8, 128), F32)
        levels = virtual_3[pl.ds(pl.multiple_of(step * 8, 8), 8), :]
        for group in range(8 // GROUP):
            parts = []
            for block in range(group * GROUP, group * GROUP + GROUP):
                at = pl.multiple_of(step * TM + block * 128, 128)
                b = step * 8 + block
                at1 = pl.ds(pl.multiple_of(b * 64, 64), 64)
                at2 = pl.ds(pl.multiple_of(b * 32, 32), 32)
                at3 = pl.ds(pl.multiple_of(b * 16, 16), 16)
                bias = None
                if block == 0:
                    bias = jnp.where(iota((1, 384), 1) < 128, first, 0.0)
                    before = pl.multiple_of(jnp.maximum(at - 128, 0), 128)
                    window = jnp.concatenate(
                        [jnp.where(step == 0, above, kv[pl.ds(before, 128), :]), kv[pl.ds(at, 256), :]], 0
                    )
                elif block == 7:
                    after = pl.multiple_of(jnp.minimum(at + 128, TOKENS - 128), 128)
                    window = jnp.concatenate(
                        [
                            kv[pl.ds(pl.multiple_of(at - 128, 128), 256), :],
                            jnp.where(step == RUNS - 1, below, kv[pl.ds(after, 128), :]),
                        ],
                        0,
                    )
                else:
                    window = kv.at[pl.ds(pl.multiple_of(at - 128, 128), 384)]
                if block == 7:
                    bias = jnp.where(iota((1, 384), 1) >= 256, last, 0.0)
                for head in range(HEADS):
                    c, gv = (slice(i * 256 + head * 128, i * 256 + head * 128 + 128) for i in range(2))
                    values = jnp.concatenate(
                        [o1[at1, c], o2[at2, c], o3[at3, c], jnp.zeros((16, DH), BF)], 0
                    )
                    parts.append(
                        (
                            q[pl.ds(at, 128), c],
                            window[:, c],
                            window[:, gv],
                            levels[block : block + 1, c],
                            values,
                            bias,
                        )
                    )
            done = merged(parts, found)
            for index, block in enumerate(range(group * GROUP, group * GROUP + GROUP)):
                sums = jnp.zeros((128, DH), F32)
                at = pl.ds(pl.multiple_of(step * TM + block * 128, 128), 128)
                for head in range(HEADS):
                    weighted, total, _ = done[index * HEADS + head]
                    attention = quotient(weighted, total)
                    out[at, head * 128 : head * 128 + 128] = attention.astype(BF)
                    sums = sums + attention * attention
                token_sums = dot_t(jnp.ones((8, DH), F32), sums)
                gathered = jnp.where(row == block, token_sums, gathered)
        squares[pl.ds(pl.multiple_of(step * 8, 8), 8), :] = gathered


def fine(edge, *arrays):
    local = pl.BlockSpec(memory_space=pltpu.VMEM)
    shape = jax.ShapeDtypeStruct
    return pl.pallas_call(
        fine_kernel,
        in_specs=[pl.BlockSpec(memory_space=pltpu.SMEM)] + [local] * len(arrays),
        out_specs=[local, local],
        scratch_shapes=[pltpu.VMEM((512, 256), BF), pltpu.VMEM((32, 256), F32)],
        out_shape=[shape((TOKENS, 256), BF), shape((32, 128), F32)],
        compiler_params=pltpu.CompilerParams(vmem_limit_bytes=VMEM_LIMIT),
        name="merge_levels",
        cost_estimate=pl.CostEstimate(
            flops=4 * TOKENS * 512 * 256, bytes_accessed=18 * 2**20, transcendentals=TOKENS * 1024
        ),
    )(edge, *arrays)


def norm_kernel(rows, s0, s1, s2, s3, gain, out, done, out_sem):
    leaving = parts_of(done, out, out_sem, 8)
    total = s0[...] + s1[...] + s2[...] + s3[...]
    factor = lax.rsqrt(total / D + 1e-6)
    eye = iota((128, 128), 0) == iota((128, 128), 1)
    for part in range(8):
        for block in range(part * 4, part * 4 + 4):
            mine = slice(block * 128, block * 128 + 128)
            column = jnp.sum(jnp.where(eye, factor[block : block + 1], 0.0), axis=1, keepdims=True)
            done[mine, :] = (rows[mine, :].astype(F32) * column * gain[...]).astype(BF)
        leaving[part].start()
    wait_all(leaving)


def norm(attention, sums, gain):
    local = pl.BlockSpec(memory_space=pltpu.VMEM)
    return pl.pallas_call(
        norm_kernel,
        in_specs=[local] * 6,
        out_specs=pl.BlockSpec(memory_space=pl.ANY),
        out_shape=jax.ShapeDtypeStruct((TOKENS, 256), BF),
        scratch_shapes=[pltpu.VMEM((TOKENS, 256), BF), pltpu.SemaphoreType.DMA((8,))],
        compiler_params=pltpu.CompilerParams(vmem_limit_bytes=16 * 2**20),
        name="norm",
    )(attention, *sums, gain)


def join_kernel(a, b, c, out):
    out[:, :256] = a[...]
    out[:, 256:512] = b[...]
    out[:, 512:] = c[...]


def joined(*weights):
    local = pl.BlockSpec(memory_space=pltpu.VMEM)
    return pl.pallas_call(
        join_kernel,
        in_specs=[local] * 3,
        out_specs=local,
        out_shape=jax.ShapeDtypeStruct((128, 768), BF),
        name="join_weights",
    )(*weights)


def shards(hidden_states, w_query, w_key, w_value, norm_gain):
    position = lax.axis_index("seq")
    core = lax.axis_index("head") % 2
    x, z = position // SIDE, position % SIDE
    w_mine = joined(w_key, w_value, w_query)
    line = jnp.stack([w_mine] + [along_line(w_mine, True, s) for s in SHIFTS])
    pieces = [line] + [along_line(line, False, s) for s in SHIFTS[:2]]
    *pieces, line = lax.optimization_barrier((*pieces, line))
    pieces = [*pieces, along_line(line, False, SHIFTS[2])]
    back = jnp.array((0,) + SHIFTS, jnp.int32)
    near_x = jnp.where(core == 0, (x - back[:, None]) % SIDE, (x - back[None, :]) % SIDE)
    near_z = jnp.where(core == 0, (z - back[None, :]) % SIDE, (z - back[:, None]) % SIDE)
    place = jnp.concatenate([(near_x * SIDE + near_z).reshape(16), (position % 2).reshape(1)])
    place = place.astype(jnp.int32)
    sums, rest = project_early(place, hidden_states, pieces[:3])
    kv, kv1, kv2, kv3, kv4, q, q1, q2, q3, q4, q5, q6, q7, send_a, send_b, send_6, send_7 = project_late(
        place, rest, pieces[3:], sums
    )
    got_d = flipped(send_7, 4)
    got_a = flipped(send_a, 1)
    got_b = other_side(send_b)
    far = jnp.concatenate([send_6, got_d], 0)
    got_s = flipped(got_d, 1)
    got_c = flipped(far, 2)
    got_e = flipped(far, 3)
    o1, o2, virtual = pairs(q1, kv1, q2, kv2)
    edge = jnp.stack([position % 2, position == 0, position == 15]).astype(jnp.int32)
    attention, squares = fine(
        edge, q3, kv3, q4, kv4, q5, q6, q7, got_a, got_b, got_d, got_s, got_c, got_e, virtual, q, kv, o1, o2
    )
    chip = squares + over_heads(squares, lambda i: i ^ 1)
    sums = [chip] + [over_heads(chip, lambda i, s=s: (i + 2 * s) % 8) for s in SHIFTS]
    return norm(attention, sums, norm_gain.reshape(1, 256))


def solution(mesh):
    in_specs = (P("seq", None), P("seq", "head"), P("seq", "head"), P("seq", "head"), P("head"))
    return jax.shard_map(
        shards, mesh=mesh, in_specs=in_specs, out_specs=P("seq", "head"), check_vma=False
    )
```

```python
import jax
import jax.numpy as jnp
import numpy as np
from jax import lax
from jax.experimental import pallas as pl
from jax.experimental.pallas import tpu as pltpu
from jax.sharding import PartitionSpec as P

H = 16
DH = 128
B = 128
D = 2048
HEADS = 2
SIDE = 4
TOKENS = 4096
SCALE = float(DH**-0.5 * np.log2(np.e))
GONE = -1e30
SHIFTS = (1, 3, 2)
BF = jnp.bfloat16
F32 = jnp.float32
TM = 1024
CHUNK = 1024
CHUNKS = TOKENS // CHUNK
RUNS = TOKENS // TM
VMEM_LIMIT = 32 * 2**20
EARLY_LIMIT = 28 * 2**20
LATE_LIMIT = 20 * 2**20
GROUP = 8


def line_perm(first, shift):
    pairs = []
    for x in range(SIDE):
        for z in range(SIDE):
            for head in range(8):
                if (head % 2 == 0) == first:
                    target = x * SIDE + (z + shift) % SIDE
                else:
                    target = (x + shift) % SIDE * SIDE + z
                pairs.append(((x * SIDE + z) * 8 + head, target * 8 + head))
    return pairs


def along_line(value, first, shift):
    return lax.ppermute(value, ("seq", "head"), line_perm(first, shift))


def flipped(value, bits):
    return lax.ppermute(value, "seq", [(i, i ^ bits) for i in range(16)])


def other_side(value):
    pairs = [(i, i + 1) for i in range(1, 15, 2)] + [(i + 1, i) for i in range(1, 15, 2)]
    return lax.ppermute(value, "seq", pairs)


def over_heads(value, step):
    return lax.ppermute(value, "head", [(i, step(i)) for i in range(8)])


def dot(a, b):
    return lax.dot_general(a, b, (((1,), (0,)), ((), ())), preferred_element_type=F32)


def dot_t(a, b):
    return lax.dot_general(a, b, (((1,), (1,)), ((), ())), preferred_element_type=F32)


def iota(shape, dim):
    return lax.broadcasted_iota(jnp.int32, shape, dim)


def level_matches(rows, first, levels, row_dim):
    shape = (128, rows) if row_dim == 1 else (rows, rows)
    token, slot = iota(shape, 0), iota(shape, 1)
    found = jnp.zeros(shape, jnp.bool_)
    start = 0
    for level in levels:
        count = 128 >> (level - first + 1)
        found = found | ((slot - start) == (token >> (level - first + 1)))  & (slot >= start) & (
            slot < start + count
        )
        start += count
    return found


def pool_matrix(rows, tokens, levels, first=0):
    row, token = iota((rows, tokens), 0), iota((rows, tokens), 1)
    total = jnp.zeros((rows, tokens), F32)
    start = 0
    for level in levels:
        count = tokens >> (level - first)
        inside = (row >= start) & (row < start + count) & ((row - start) == (token >> (level - first)))
        total = jnp.where(inside, 2.0 ** (first - level), total)
        start += count
    return total.astype(BF)


def parts_of(source, target, sems, count):
    rows = source.shape[0] // count
    return [
        pltpu.make_async_copy(
            source.at[pl.ds(i * rows, rows)], target.at[pl.ds(i * rows, rows)], sems.at[i]
        )
        for i in range(count)
    ]


def part_of(source, target, sems, index, rows):
    at = pl.ds(pl.multiple_of(index * rows, rows), rows)
    return pltpu.make_async_copy(source.at[at], target.at[at], sems.at[index])


def start_all(copies):
    for copy in copies:
        copy.start()


def wait_all(copies):
    for copy in copies:
        copy.wait()


def half_rows(place, base, hidden, ring, h_sem, index):
    rows = pl.ds(pl.multiple_of(index * CHUNK, CHUNK), CHUNK)
    slot = index % 3
    return [
        pltpu.make_async_copy(
            hidden.at[rows, pl.ds(pl.multiple_of(place[base + block] * 128, 128), 128)],
            ring.at[slot, :, pl.ds(block * 128, 128)],
            h_sem.at[slot, block],
        )
        for block in range(ring.shape[2] // 128)
    ]


def next_half(place, base, hidden, ring, h_sem, index):
    wait_all(half_rows(place, base, hidden, ring, h_sem, index))

    @pl.when(index < CHUNKS - 2)
    def _():
        start_all(half_rows(place, base, hidden, ring, h_sem, index + 2))


def join_half(pieces, w_half):
    for n, piece in enumerate(pieces):
        for i in range(SIDE):
            w_half[(n * SIDE + i) * 128 : (n * SIDE + i + 1) * 128, :] = piece[i]


def pool_runs(l3):
    p_coarse = pool_matrix(128, 128, (4, 5, 6, 7), 3)
    coarse = [dot(p_coarse, l3[run * 128 : run * 128 + 128, :]) for run in range(4)]
    return [
        jnp.concatenate([c[low:high] for c in coarse], 0).astype(BF)
        for low, high in ((0, 64), (64, 96), (96, 112), (112, 120))
    ]


def fetch_kernel(place, hidden, ready, first, sems):
    copies = [
        pltpu.make_async_copy(
            hidden.at[pl.ds(0, CHUNK), pl.ds(pl.multiple_of(place[block] * 128, 128), 128)],
            first.at[:, pl.ds(block * 128, 128)],
            sems.at[block],
        )
        for block in range(12)
    ]
    start_all(copies)
    wait_all(copies)


def fetch(place, hidden, ready):
    anywhere = pl.BlockSpec(memory_space=pl.ANY)
    return pl.pallas_call(
        fetch_kernel,
        in_specs=[pl.BlockSpec(memory_space=pltpu.SMEM), anywhere, anywhere],
        out_specs=pl.BlockSpec(memory_space=pltpu.VMEM),
        out_shape=jax.ShapeDtypeStruct((CHUNK, 1536), BF),
        scratch_shapes=[pltpu.SemaphoreType.DMA((12,))],
        compiler_params=pltpu.CompilerParams(vmem_limit_bytes=8 * 2**20),
        name="fetch_first",
        cost_estimate=pl.CostEstimate(flops=0, bytes_accessed=3 * 2**20, transcendentals=0),
    )(place, hidden, ready)


def early_kernel(place, hidden, first, w0, w1, w2, sums, rest, ring, w_half, h_sem, rest_sem):
    for index in range(1, 3):
        start_all(half_rows(place, 0, hidden, ring, h_sem, jnp.int32(index)))
    join_half((w0, w1, w2), w_half)
    columns = [
        pltpu.make_async_copy(
            hidden.at[:, pl.ds(pl.multiple_of(place[12 + block] * 128, 128), 128)],
            rest.at[:, pl.ds(block * 128, 128)],
            rest_sem.at[block],
        )
        for block in range(SIDE)
    ]

    sums[:CHUNK, :] = dot(first[...], w_half[...]).astype(BF)

    @pl.loop(1, CHUNKS)
    def _(index):
        next_half(place, 0, hidden, ring, h_sem, index)

        @pl.when(index == CHUNKS - 2)
        def _():
            start_all(columns)

        at = pl.ds(pl.multiple_of(index * CHUNK, CHUNK), CHUNK)
        sums[at, :] = dot(ring[index % 3], w_half[...]).astype(BF)

    wait_all(columns)


def late_kernel(
    place, rest, w3, sums,
    kv, kv1, kv2, kv3, kv4, q, q1, q2, q3, q4, q5, q6, q7, send_a, send_b, six, seven,
    w_half, l3,
):
    join_half((w3,), w_half)
    p_fine = pool_matrix(112, 128, (1, 2, 3))

    def pool(index):
        at = pl.ds(pl.multiple_of(index * CHUNK, CHUNK), CHUNK)
        rows = jnp.concatenate([kv[at, :], q[at, :]], 1)
        pooled = [
            dot(p_fine, rows[part * 128 : part * 128 + 128]).astype(BF) for part in range(CHUNK // 128)
        ]
        for part, means in enumerate(pooled):
            block = index * (CHUNK // 128) + part
            at1 = pl.ds(pl.multiple_of(block * 64, 64), 64)
            at2 = pl.ds(pl.multiple_of(block * 32, 32), 32)
            at3 = pl.ds(pl.multiple_of(block * 16, 16), 16)
            kv1[at1, :] = means[:64, :512]
            q1[at1, :] = means[:64, 512:]
            kv2[at2, :] = means[64:96, :512]
            q2[at2, :] = means[64:96, 512:]
            l3[at3, :] = means[96:112]

    def project(index):
        at = pl.ds(pl.multiple_of(index * CHUNK, CHUNK), CHUNK)
        rows = (dot(rest[at, :], w_half[...]) + sums[at, :].astype(F32)).astype(BF)
        return at, rows

    at, rows = project(jnp.int32(0))
    kv[at, :] = rows[:, :512]
    q[at, :] = rows[:, 512:]

    @pl.loop(1, CHUNKS)
    def _(index):
        at, rows = project(index)
        pool(index - 1)
        kv[at, :] = rows[:, :512]
        q[at, :] = rows[:, 512:]

    pool(CHUNKS - 1)
    kv3[...] = l3[:, :512]
    q3[...] = l3[:, 512:]
    four, five, last, tail = pool_runs(l3)
    kv4[...] = four[:, :512]
    q4[...] = four[:, 512:]
    q5[...] = five[:, 512:]
    q6[...] = last[:, 512:]
    q7[...] = tail[:, 512:]
    six[...] = last[:, :512]
    seven[...] = tail[:, :512]
    odd = place[16] == 1
    low, high = kv[:128, :], kv[TOKENS - 128 :, :]
    send_a[:128, :] = jnp.where(odd, low, high)
    send_b[...] = jnp.where(odd, high, low)
    send_a[128:, :] = five[:, :512]


def project_early(place, hidden, first, pieces):
    anywhere = pl.BlockSpec(memory_space=pl.ANY)
    local = pl.BlockSpec(memory_space=pltpu.VMEM)
    return pl.pallas_call(
        early_kernel,
        in_specs=[pl.BlockSpec(memory_space=pltpu.SMEM), anywhere] + [local] * 4,
        out_specs=[local, local],
        out_shape=[jax.ShapeDtypeStruct((TOKENS, 768), BF), jax.ShapeDtypeStruct((TOKENS, 512), BF)],
        scratch_shapes=[
            pltpu.VMEM((3, CHUNK, 1536), BF),
            pltpu.VMEM((1536, 768), BF),
            pltpu.SemaphoreType.DMA((3, 12)),
            pltpu.SemaphoreType.DMA((SIDE,)),
        ],
        compiler_params=pltpu.CompilerParams(vmem_limit_bytes=EARLY_LIMIT),
        name="project_early",
        cost_estimate=pl.CostEstimate(
            flops=3 * TOKENS * 1024 * 768, bytes_accessed=12 * 2**20, transcendentals=0
        ),
    )(place, hidden, first, *pieces)


def project_late(place, rest, pieces, sums):
    local = pl.BlockSpec(memory_space=pltpu.VMEM)
    sizes = [(TOKENS >> level, 512) for level in range(5)]
    sizes += [(TOKENS >> level, 256) for level in range(8)]
    sizes += [(256, 512), (128, 512), (64, 512), (32, 512)]
    return pl.pallas_call(
        late_kernel,
        in_specs=[pl.BlockSpec(memory_space=pltpu.SMEM)] + [local] * 3,
        out_specs=[local] * len(sizes),
        out_shape=[jax.ShapeDtypeStruct(size, BF) for size in sizes],
        scratch_shapes=[
            pltpu.VMEM((512, 768), BF),
            pltpu.VMEM((512, 768), BF),
        ],
        compiler_params=pltpu.CompilerParams(vmem_limit_bytes=LATE_LIMIT),
        name="project_late",
        cost_estimate=pl.CostEstimate(
            flops=TOKENS * 1024 * 768, bytes_accessed=8 * 2**20, transcendentals=0
        ),
    )(place, rest, *pieces, sums)


def pairs_kernel(q1, kv1, q2, kv2, o1, o2, virtual):
    for run in range(RUNS):
        triples, places = [], []
        for head in range(HEADS):
            k, v = (slice(i * 256 + head * 128, i * 256 + head * 128 + 128) for i in range(2))
            for q_all, kv_all, out, count in ((q1, kv1, o1, 4), (q2, kv2, o2, 2)):
                for block in range(run * count, run * count + count):
                    mine = slice(block * 128, block * 128 + 128)
                    its = slice((block ^ 1) * 128, (block ^ 1) * 128 + 128)
                    triples.append((q_all[mine, k], kv_all[its, k], kv_all[its, v]))
                    places.append((out, mine, k))
        done = attend_all(triples)
        for (out, mine, k), (rows, _) in zip(places, done):
            out[mine, k] = rows
        for head in range(HEADS):
            ends = [level_row(total) for _, total in done[head * 6 : head * 6 + 6]]
            lanes = []
            for block in range(8):
                fine = ends[block // 2][:, block % 2 * 64 : block % 2 * 64 + 64]
                coarse = ends[4 + block // 4][:, block % 4 * 32 : block % 4 * 32 + 32]
                lanes.append(jnp.concatenate([fine, coarse, jnp.zeros((1, 32), F32)], 1))
            virtual[run * 8 : run * 8 + 8, head * 128 : head * 128 + 128] = jnp.concatenate(lanes, 0)


def pairs(*arrays):
    local = pl.BlockSpec(memory_space=pltpu.VMEM)
    shape = jax.ShapeDtypeStruct
    return pl.pallas_call(
        pairs_kernel,
        in_specs=[local] * 4,
        out_specs=[local] * 3,
        out_shape=[shape((2048, 256), BF), shape((1024, 256), BF), shape((32, 256), F32)],
        compiler_params=pltpu.CompilerParams(vmem_limit_bytes=VMEM_LIMIT),
        name="levels_1_2",
        cost_estimate=pl.CostEstimate(
            flops=2 * 3072 * 128 * 512, bytes_accessed=9 * 2**20, transcendentals=3072 * 256
        ),
    )(*arrays)


def with_ones(values):
    return jnp.concatenate([values, jnp.ones_like(values)], axis=1)


def quotient(rows, total):
    inverse = pl.reciprocal(total, approx=True)
    return rows * (inverse * (2.0 - total * inverse))


def attend_all(triples):
    scores = [dot_t(queries, key_rows) * SCALE for queries, key_rows, _ in triples]
    highest = [jnp.max(s, axis=1, keepdims=True) for s in scores]
    weights = [jnp.exp2(s - h).astype(BF) for s, h in zip(scores, highest)]
    both = [dot(w, with_ones(values)) for w, (_, _, values) in zip(weights, triples)]
    return [
        (quotient(o[:, :DH], o[:, DH:]).astype(BF), h + jnp.log2(o[:, DH:])) for o, h in zip(both, highest)
    ]


def level_row(total):
    eye = iota((128, 128), 0) == iota((128, 128), 1)
    return jnp.sum(jnp.where(eye, total, 0.0), axis=0, keepdims=True)


def merged(parts, found):
    scores = [dot_t(queries, key_rows) * SCALE for queries, key_rows, *_ in parts]
    scores = [s if p[5] is None else s + p[5] for s, p in zip(scores, parts)]
    coarse = [jnp.where(found, p[3], GONE) for p in parts]
    highest = [
        jnp.maximum(jnp.max(s, axis=1, keepdims=True), jnp.max(c, axis=1, keepdims=True))
        for s, c in zip(scores, coarse)
    ]
    weights = [
        jnp.concatenate([jnp.exp2(s - h).astype(BF), jnp.exp2(c - h).astype(BF)], 1)
        for s, c, h in zip(scores, coarse, highest)
    ]
    both = [
        dot(w, with_ones(jnp.concatenate([p[2], p[4]], 0))) for w, p in zip(weights, parts)
    ]
    return [(o[:, :DH], o[:, DH:], h) for o, h in zip(both, highest)]


def fine_kernel(
    edge, q3, kv3, q4, kv4, q5, q6, q7, got_a, got_b, got_d, got_s, got_c, got_e, virtual, q, kv, o1, o2,
    out, squares, o3, virtual_3,
):
    odd = edge[0] == 1
    kv5 = got_a.at[pl.ds(128, 128)]
    kv6 = jnp.concatenate([got_c[:64, :], got_e[:64, :]], 0)
    kv7 = jnp.concatenate([got_d[...], got_s[...], got_c[64:, :], got_e[64:, :]], 0)
    above = jnp.where(odd, got_a[:128, :], got_b[...])
    below = jnp.where(odd, got_b[...], got_a[:128, :])
    found = level_matches(128, 4, (4, 5, 6, 7), 1)
    triples = []
    for head in range(HEADS):
        k, v = (slice(i * 256 + head * 128, i * 256 + head * 128 + 128) for i in range(2))
        for block in range(2):
            mine = slice(block * 128, block * 128 + 128)
            its = slice((block ^ 1) * 128, (block ^ 1) * 128 + 128)
            triples.append((q4[mine, k], kv4[its, k], kv4[its, v]))
        triples.append((q5[:, k], kv5[:, k], kv5[:, v]))
        triples.append((q6[:, k], kv6[:, k], kv6[:, v]))
        triples.append((q7[:, k], kv7[:, k], kv7[:, v]))
    done = attend_all(triples)
    parts = []
    for head in range(HEADS):
        k, v = (slice(i * 256 + head * 128, i * 256 + head * 128 + 128) for i in range(2))
        (oa, ea), (ob, eb), (o5, e5), (o6, e6), (o7, e7) = done[head * 5 : head * 5 + 5]
        for run in range(4):
            its = slice((run ^ 1) * 128, (run ^ 1) * 128 + 128)
            mine = slice(run * 128, run * 128 + 128)
            half = slice(run % 2 * 64, run % 2 * 64 + 64)
            values = jnp.concatenate(
                [
                    (oa, ob)[run // 2][half].astype(F32),
                    o5[run * 32 : run * 32 + 32].astype(F32),
                    o6[run * 16 : run * 16 + 16].astype(F32),
                    o7.astype(F32)[run * 8 : run * 8 + 8],
                    jnp.zeros((8, DH), F32),
                ],
                0,
            ).astype(BF)
            total = jnp.concatenate(
                [
                    (ea, eb)[run // 2][half],
                    e5[run * 32 : run * 32 + 32],
                    e6[run * 16 : run * 16 + 16],
                    e7[run * 8 : run * 8 + 8],
                    jnp.zeros((8, DH), F32),
                ],
                0,
            )
            parts.append((q3[mine, k], kv3[its, k], kv3[its, v], level_row(total), values, None))
    for index, (weighted, total, highest) in enumerate(merged(parts, found)):
        head, run = divmod(index, 4)
        c = slice(head * 128, head * 128 + 128)
        o3[run * 128 : run * 128 + 128, c] = quotient(weighted, total).astype(BF)
        ends = level_row(highest + jnp.log2(total))
        lanes = [
            jnp.concatenate(
                [jnp.zeros((1, 96), F32), ends[:, block * 16 : block * 16 + 16], jnp.zeros((1, 16), F32)], 1
            )
            for block in range(8)
        ]
        mine = slice(run * 8, run * 8 + 8)
        virtual_3[mine, c] = jnp.concatenate(lanes, 0) + virtual[mine, c]

    found = level_matches(128, 1, (1, 2, 3), 1)
    row = iota((8, 128), 0)

    @pl.loop(0, RUNS)
    def _(step):
        first = jnp.where((step == 0) & (edge[1] == 1), GONE, 0.0)
        last = jnp.where((step == 3) & (edge[2] == 1), GONE, 0.0)
        gathered = jnp.zeros((8, 128), F32)
        levels = virtual_3[pl.ds(pl.multiple_of(step * 8, 8), 8), :]
        for group in range(8 // GROUP):
            parts = []
            for block in range(group * GROUP, group * GROUP + GROUP):
                at = pl.multiple_of(step * TM + block * 128, 128)
                b = step * 8 + block
                at1 = pl.ds(pl.multiple_of(b * 64, 64), 64)
                at2 = pl.ds(pl.multiple_of(b * 32, 32), 32)
                at3 = pl.ds(pl.multiple_of(b * 16, 16), 16)
                bias = None
                if block == 0:
                    bias = jnp.where(iota((1, 384), 1) < 128, first, 0.0)
                    before = pl.multiple_of(jnp.maximum(at - 128, 0), 128)
                    window = jnp.concatenate(
                        [jnp.where(step == 0, above, kv[pl.ds(before, 128), :]), kv[pl.ds(at, 256), :]], 0
                    )
                elif block == 7:
                    after = pl.multiple_of(jnp.minimum(at + 128, TOKENS - 128), 128)
                    window = jnp.concatenate(
                        [
                            kv[pl.ds(pl.multiple_of(at - 128, 128), 256), :],
                            jnp.where(step == RUNS - 1, below, kv[pl.ds(after, 128), :]),
                        ],
                        0,
                    )
                else:
                    window = kv.at[pl.ds(pl.multiple_of(at - 128, 128), 384)]
                if block == 7:
                    bias = jnp.where(iota((1, 384), 1) >= 256, last, 0.0)
                for head in range(HEADS):
                    c, gv = (slice(i * 256 + head * 128, i * 256 + head * 128 + 128) for i in range(2))
                    values = jnp.concatenate(
                        [o1[at1, c], o2[at2, c], o3[at3, c], jnp.zeros((16, DH), BF)], 0
                    )
                    parts.append(
                        (
                            q[pl.ds(at, 128), c],
                            window[:, c],
                            window[:, gv],
                            levels[block : block + 1, c],
                            values,
                            bias,
                        )
                    )
            done = merged(parts, found)
            for index, block in enumerate(range(group * GROUP, group * GROUP + GROUP)):
                sums = jnp.zeros((128, DH), F32)
                at = pl.ds(pl.multiple_of(step * TM + block * 128, 128), 128)
                for head in range(HEADS):
                    weighted, total, _ = done[index * HEADS + head]
                    attention = quotient(weighted, total)
                    out[at, head * 128 : head * 128 + 128] = attention.astype(BF)
                    sums = sums + attention * attention
                token_sums = dot_t(jnp.ones((8, DH), F32), sums)
                gathered = jnp.where(row == block, token_sums, gathered)
        squares[pl.ds(pl.multiple_of(step * 8, 8), 8), :] = gathered


def fine(edge, *arrays):
    local = pl.BlockSpec(memory_space=pltpu.VMEM)
    shape = jax.ShapeDtypeStruct
    return pl.pallas_call(
        fine_kernel,
        in_specs=[pl.BlockSpec(memory_space=pltpu.SMEM)] + [local] * len(arrays),
        out_specs=[local, local],
        scratch_shapes=[pltpu.VMEM((512, 256), BF), pltpu.VMEM((32, 256), F32)],
        out_shape=[shape((TOKENS, 256), BF), shape((32, 128), F32)],
        compiler_params=pltpu.CompilerParams(vmem_limit_bytes=VMEM_LIMIT),
        name="merge_levels",
        cost_estimate=pl.CostEstimate(
            flops=4 * TOKENS * 512 * 256, bytes_accessed=18 * 2**20, transcendentals=TOKENS * 1024
        ),
    )(edge, *arrays)


def norm_kernel(rows, s0, s1, s2, s3, gain, out, done, out_sem):
    leaving = parts_of(done, out, out_sem, 8)
    total = s0[...] + s1[...] + s2[...] + s3[...]
    factor = lax.rsqrt(total / D + 1e-6)
    eye = iota((128, 128), 0) == iota((128, 128), 1)
    for part in range(8):
        for block in range(part * 4, part * 4 + 4):
            mine = slice(block * 128, block * 128 + 128)
            column = jnp.sum(jnp.where(eye, factor[block : block + 1], 0.0), axis=1, keepdims=True)
            done[mine, :] = (rows[mine, :].astype(F32) * column * gain[...]).astype(BF)
        leaving[part].start()
    wait_all(leaving)


def norm(attention, sums, gain):
    local = pl.BlockSpec(memory_space=pltpu.VMEM)
    return pl.pallas_call(
        norm_kernel,
        in_specs=[local] * 6,
        out_specs=pl.BlockSpec(memory_space=pl.ANY),
        out_shape=jax.ShapeDtypeStruct((TOKENS, 256), BF),
        scratch_shapes=[pltpu.VMEM((TOKENS, 256), BF), pltpu.SemaphoreType.DMA((8,))],
        compiler_params=pltpu.CompilerParams(vmem_limit_bytes=16 * 2**20),
        name="norm",
    )(attention, *sums, gain)


def join_kernel(a, b, c, out):
    out[:, :256] = a[...]
    out[:, 256:512] = b[...]
    out[:, 512:] = c[...]


def joined(*weights):
    local = pl.BlockSpec(memory_space=pltpu.VMEM)
    return pl.pallas_call(
        join_kernel,
        in_specs=[local] * 3,
        out_specs=local,
        out_shape=jax.ShapeDtypeStruct((128, 768), BF),
        name="join_weights",
    )(*weights)


def shards(hidden_states, w_query, w_key, w_value, norm_gain):
    position = lax.axis_index("seq")
    core = lax.axis_index("head") % 2
    x, z = position // SIDE, position % SIDE
    w_mine = joined(w_key, w_value, w_query)
    line = jnp.stack([w_mine] + [along_line(w_mine, True, s) for s in SHIFTS])
    pieces = [line] + [along_line(line, False, s) for s in SHIFTS[:2]]
    back = jnp.array((0,) + SHIFTS, jnp.int32)
    near_x = jnp.where(core == 0, (x - back[:, None]) % SIDE, (x - back[None, :]) % SIDE)
    near_z = jnp.where(core == 0, (z - back[None, :]) % SIDE, (z - back[:, None]) % SIDE)
    place = jnp.concatenate([(near_x * SIDE + near_z).reshape(16), (position % 2).reshape(1)])
    place = place.astype(jnp.int32)
    first = fetch(place, hidden_states, line)
    near, ready, first = lax.optimization_barrier((pieces[2], line, first))
    pieces = [line, pieces[1], near, along_line(ready, False, SHIFTS[2])]
    sums, rest = project_early(place, hidden_states, first, pieces[:3])
    kv, kv1, kv2, kv3, kv4, q, q1, q2, q3, q4, q5, q6, q7, send_a, send_b, send_6, send_7 = project_late(
        place, rest, pieces[3:], sums
    )
    got_d = flipped(send_7, 4)
    got_a = flipped(send_a, 1)
    got_b = other_side(send_b)
    far = jnp.concatenate([send_6, got_d], 0)
    got_s = flipped(got_d, 1)
    got_c = flipped(far, 2)
    got_e = flipped(far, 3)
    o1, o2, virtual = pairs(q1, kv1, q2, kv2)
    edge = jnp.stack([position % 2, position == 0, position == 15]).astype(jnp.int32)
    attention, squares = fine(
        edge, q3, kv3, q4, kv4, q5, q6, q7, got_a, got_b, got_d, got_s, got_c, got_e, virtual, q, kv, o1, o2
    )
    chip = squares + over_heads(squares, lambda i: i ^ 1)
    sums = [chip] + [over_heads(chip, lambda i, s=s: (i + 2 * s) % 8) for s in SHIFTS]
    return norm(attention, sums, norm_gain.reshape(1, 256))


def solution(mesh):
    in_specs = (P("seq", None), P("seq", "head"), P("seq", "head"), P("seq", "head"), P("head"))
    return jax.shard_map(
        shards, mesh=mesh, in_specs=in_specs, out_specs=P("seq", "head"), check_vma=False
    )
```
